128 devices in a mesh: row: 16 (over z, x), col: 8 (over y, core).
Axes of the slice: x: 4, y: 4, z: 4, core: 2. Of those that a mesh axis runs over, the one named last changes fastest.
Arguments:
- points: float32 [8, 65536], P(None, ('row', 'col')), may hold values from -5 to 5
- lengthscale: float32 [8], replicated, may hold values from 0.6 to 1.6
- outputscale: float32 [1], replicated, may hold values from 0.5 to 1.5
- noise: float32 [1], replicated, may hold values from 0.1 to 0.6
- solution: float32 [8, 65536], P(None, ('row', 'col')), may hold values from -6 to 6
- residual: float32 [8, 65536], P(None, ('row', 'col')), may hold values from -6 to 6
- direction: float32 [8, 65536], P(None, ('row', 'col')), may hold values from -12 to 12
Outputs:
- new_solution: float32 [8, 65536], P(None, ('row', 'col'))
- new_residual: float32 [8, 65536], P(None, ('row', 'col'))
- new_direction: float32 [8, 65536], P(None, ('row', 'col'))
The draws below stay inside these ranges and needn't reach their ends.
All inputs are finite; a program needn't handle non-finite values.
Results may differ from the reference program's by a relative error of at most 0.000065.
Values sent between devices are 32-bit elements; how exact they have to be, the bound alone decides.
No kernel may reach another device: no remote copies, remote signals or barrier semaphores. Data moves between devices by JAX's collectives and lax.ppermute only.
A program may use at most 64 MiB of HBM per device.

```python
import math
import jax
import jax.numpy as jnp
from jax import lax

FEAT = 8
COLS = 8
PTS_DEV = 512
POINTS = 65536
DEVICES = 128


def draw_direction(key, part):
    key = jax.random.fold_in(key, 3)
    rising = 1.0 + 2.0 * jnp.arange(POINTS, dtype=jnp.float32) / (POINTS - 1)
    base = jnp.clip(jax.random.normal(key, (COLS, POINTS), jnp.float32), -4.0, 4.0)
    return base * rising[None, :]


def block_scale(own_key, extent, cuts, smallest, largest):
    gain = 1.0
    for position, blocks in cuts:
        draws = jax.random.uniform(jax.random.fold_in(jax.random.fold_in(own_key, 6), position), (blocks,), jnp.float32, smallest / len(cuts), largest / len(cuts))
        gain = gain * jnp.repeat(jnp.exp(draws), extent[position] // blocks).reshape((-1,) + (1,) * (len(extent) - 1 - position))
    return gain


def bell_draw(own_key, extent, spread, reach, cuts=(), kind=jnp.bfloat16):
    drawn = jax.random.normal(own_key, extent, jnp.float32) * spread
    if len(cuts) > 0:
        drawn = block_scale(own_key, extent, cuts, -0.22, 0.18) * drawn
    return jnp.clip(drawn, min=-reach, max=reach).astype(kind)


def setup_inputs(seed: int = 0) -> dict:
    key_of = jax.random.split(jax.random.key(seed), 8)
    return {
        "points": bell_draw(key_of[0], (FEAT, POINTS), 1.0, 5.0, ((1, 128),), jnp.float32),
        "lengthscale": jnp.clip(jnp.exp(jax.random.uniform(key_of[1], (FEAT,), jnp.float32, math.log(0.6), math.log(1.6))), 0.6, 1.6),
        "outputscale": jnp.clip(jax.random.uniform(key_of[2], (1,), jnp.float32, 0.5, 1.5), 0.5, 1.5),
        "noise": jnp.clip(jax.random.uniform(key_of[3], (1,), jnp.float32, 0.1, 0.6), 0.1, 0.6),
        "solution": bell_draw(key_of[4], (COLS, POINTS), 1.0, 6.0, ((1, 128),), jnp.float32),
        "residual": bell_draw(key_of[5], (COLS, POINTS), 1.0, 6.0, ((1, 128),), jnp.float32),
        "direction": draw_direction(jax.random.fold_in(key_of[7], 71), 0),
    }


def matern(left, right, outputscale):
    cross = jnp.dot(left.T, right, precision=lax.Precision.HIGHEST, preferred_element_type=jnp.float32)
    left_sq = lax.optimization_barrier(jnp.sum(left * left, axis=0))
    right_sq = lax.optimization_barrier(jnp.sum(right * right, axis=0))
    dist_sq = jnp.maximum(left_sq[:, None] + right_sq[None, :] - 2.0 * cross, 0.0)
    radius = jnp.sqrt(dist_sq)
    root_five = 5.0 ** 0.5
    return outputscale * (1.0 + root_five * radius + 5.0 / 3.0 * dist_sq) * jnp.exp(-root_five * radius)

def reference(points, lengthscale, outputscale, noise, solution, residual, direction):
    scaled = points / lengthscale[:, None]

    def row_block(index):
        left = lax.dynamic_slice_in_dim(scaled, index * PTS_DEV, PTS_DEV, 1)
        tiles = matern(left, scaled, outputscale[0])
        return jnp.dot(direction, tiles.T, precision=lax.Precision.HIGHEST, preferred_element_type=jnp.float32)
    pieces = lax.map(row_block, jnp.arange(DEVICES, dtype=jnp.int32))
    product = jnp.transpose(pieces, (1, 0, 2)).reshape(COLS, POINTS)
    image = product + noise[0] * direction
    rr_old = lax.optimization_barrier(jnp.sum(residual * residual, axis=1))
    curv = lax.optimization_barrier(jnp.sum(direction * image, axis=1))
    alpha = rr_old / curv
    new_solution = solution + alpha[:, None] * direction
    new_residual = residual - alpha[:, None] * image
    rr_new = lax.optimization_barrier(jnp.sum(new_residual * new_residual, axis=1))
    new_direction = new_residual + (rr_new / rr_old)[:, None] * direction
    return (new_solution, new_residual, new_direction)
```

```python
import jax
import jax.numpy as jnp
from jax import lax
from jax.experimental import pallas as pl
from jax.experimental.pallas import tpu as pltpu
from jax.sharding import PartitionSpec as P

width = 512
per_group = 8
groups = 16
group_pts = width * per_group
depth = 64
chunk = 128
steps = 65
pts_scale = 5.0**0.5 / 3.0
f32, bf16 = jnp.float32, jnp.bfloat16
nt_dims = (((1,), (1,)), ((), ()))
both = ("row", "col")


def dot(left, right):
    return jnp.dot(left, right, preferred_element_type=f32)


def split(value, parts):
    out = []
    for _ in range(parts):
        top = value.astype(bf16).astype(f32)
        out.append(top)
        value = value - top
    return out


def send_kernel(pts_ref, len_ref, dir_ref, out_ref):
    rows = lax.broadcasted_iota(jnp.int32, pts_ref.shape, 0)
    lengths = jnp.zeros(pts_ref.shape, f32)
    for feat in range(8):
        lengths = jnp.where(rows == feat, len_ref[feat], lengths)
    scaled = pts_ref[...] / lengths * pts_scale
    for block in range(per_group):
        out_ref[block, 0:8, :] = scaled
        out_ref[block, 8:16, :] = dir_ref[...]


def norm_rows(pts, first):
    rows = lax.broadcasted_iota(jnp.int32, pts.shape, 0)
    out = jnp.where(rows < 6, 1.0, 0.0)
    for i, part in enumerate(split(jnp.sum(pts * pts, axis=0, keepdims=True), 3)):
        out = jnp.where(rows == first + i, part, out)
    return out


def right_rows(pts):
    one, two, three = split(pts, 3)
    return jnp.concatenate(
        [one, two, one, three, two, one, norm_rows(pts, 3), jnp.zeros_like(pts)], axis=0
    )


def left_rows(pts):
    one, two, three = split(pts * -2.0, 3)
    return jnp.concatenate(
        [one, one, two, one, two, three, norm_rows(pts, 0), jnp.zeros_like(pts)], axis=0
    )


def right_and_dir(block, right_ref, dir_ref, at):
    cols = slice(at * width, (at + 1) * width)
    right_ref[:, cols] = right_rows(block[0:8, :]).astype(bf16)
    dir_ref[:, cols] = jnp.concatenate(split(block[8:16, :], 2), axis=0).astype(bf16)


def own_kernel(own_ref, left_ref, right_ref, dir_ref):
    for at in range(per_group):
        block = own_ref[at]
        left_ref[at * width : (at + 1) * width, :] = left_rows(block[0:8, :]).T.astype(bf16)
        right_and_dir(block, right_ref, dir_ref, at)


def matern(dist):
    dist = jnp.maximum(dist, 1e-30)
    radius = dist * lax.rsqrt(dist)
    decay = jnp.exp2(radius * (-3.0 / 0.6931471805599453))
    return ((dist + 1.0 / 3.0) + radius) * decay


def tile_of(step, group, col):
    pair_row, pair_col = step // 8, 8 + step % 8
    last = step == 64
    diag = jnp.where(col <= 3, 4 + col, 0)
    pair_weight = jnp.where(last, jnp.where(col <= 3, 0.5, 0.0), 1.0)
    pair_row, pair_col = jnp.where(last, diag, pair_row), jnp.where(last, diag, pair_col)
    half_row = step // 4
    half_col = 8 + 2 * (step % 4) + (half_row + group // 8) % 2
    inner = step - 32
    shift = 1 + inner // 8
    on_diag = inner >= 28
    inner_row = jnp.where(on_diag, inner - 28, inner % 8)
    inner_col = jnp.where(on_diag, inner_row, (inner_row + shift) % 8)
    first = step < 32
    own_row = jnp.where(first, half_row, inner_row)
    own_col = jnp.where(first, half_col, inner_col)
    own_weight = jnp.where(on_diag, 0.5, 1.0)
    own = col == 0
    return (
        jnp.where(own, own_row, pair_row),
        jnp.where(own, own_col, pair_col),
        jnp.where(own, own_weight, pair_weight),
    )


def pair_kernel(place_ref, left_ref, own_right_ref, own_dir_ref, other_ref, own_out, other_out,
                right_ref, dir_ref, acc_ref, top_even, low_even, top_odd, low_odd):
    group, col = place_ref[0], place_ref[1]
    right_ref[:, :group_pts] = own_right_ref[...]
    dir_ref[:, :group_pts] = own_dir_ref[...]
    for at in range(per_group):
        right_and_dir(other_ref[at], right_ref, dir_ref, per_group + at)
    acc_ref[...] = jnp.zeros_like(acc_ref)

    def evaluate(step, top, low):
        row, column, _ = tile_of(step, group, col)
        row, column = pl.multiple_of(row * width, width), pl.multiple_of(column * width, width)

        def part(at):
            rows = slice(at * chunk, (at + 1) * chunk)
            tile = matern(
                dot(left_ref[pl.ds(row + at * chunk, chunk), :], right_ref[:, pl.ds(column, width)])
            )
            high = tile.astype(bf16)
            top[rows, :] = high
            low[rows, :] = (tile - high.astype(f32)).astype(bf16)

        return [lambda at=at: part(at) for at in range(width // chunk)]

    def multiply(step, top, low):
        row, column, weight = tile_of(step, group, col)
        row, column = pl.multiple_of(row * width, width), pl.multiple_of(column * width, width)

        def to_column(tile):
            acc_ref[:, pl.ds(column, width)] += weight * dot(
                dir_ref[:, pl.ds(row, width)], tile[...]
            )

        def to_row(tile):
            acc_ref[:, pl.ds(row, width)] += weight * lax.dot_general(
                dir_ref[:, pl.ds(column, width)], tile[...], nt_dims, preferred_element_type=f32
            )

        return [
            lambda: to_column(top), lambda: to_column(low), lambda: to_row(top), lambda: to_row(low)
        ]

    def run(first, second):
        for one, two in zip(first, second, strict=True):
            one()
            two()

    for part in evaluate(0, top_even, low_even):
        part()

    def turn(index, carry):
        step = 2 * index
        run(evaluate(step + 1, top_odd, low_odd), multiply(step, top_even, low_even))
        run(evaluate(step + 2, top_even, low_even), multiply(step + 1, top_odd, low_odd))
        return carry

    lax.fori_loop(0, steps // 2, turn, 0)
    for part in multiply(steps - 1, top_even, low_even):
        part()
    for at in range(per_group):
        cols = slice(at * width, (at + 1) * width)
        own_out[at] = acc_ref[0:8, cols] + acc_ref[8:16, cols]
        cols = slice(group_pts + at * width, group_pts + (at + 1) * width)
        other_out[at] = acc_ref[0:8, cols] + acc_ref[8:16, cols]


def image_kernel(scale_ref, noise_ref, parts_ref, dir_ref, res_ref, image_ref, sums_ref):
    product = parts_ref[0]
    for at in range(1, per_group):
        product = product + parts_ref[at]
    direction, residual = dir_ref[...], res_ref[...]
    image = (3.0 * scale_ref[0]) * product + noise_ref[0] * direction
    image_ref[...] = image
    rows = lax.broadcasted_iota(jnp.int32, (8, 128), 0)
    lanes = lax.broadcasted_iota(jnp.int32, (8, 128), 1)
    packed = jnp.zeros((8, 128), f32)
    pairs = ((residual, residual), (direction, image), (residual, image), (image, image))
    for i, (one, two) in enumerate(pairs):
        packed = jnp.where(lanes == 8 * i + rows, jnp.sum(one * two, axis=1, keepdims=True), packed)
    sums_ref[...] = jnp.broadcast_to(jnp.sum(packed, axis=0, keepdims=True), sums_ref.shape)


def update_kernel(sums_ref, image_ref, sol_ref, res_ref, dir_ref, new_sol, new_res, new_dir):
    total = jnp.sum(sums_ref[...], axis=0, keepdims=True)
    rows = lax.broadcasted_iota(jnp.int32, (8, 128), 0)
    lanes = lax.broadcasted_iota(jnp.int32, (8, 128), 1)
    rr_old, curv, res_image, image_sq = (
        jnp.sum(jnp.where(lanes == 8 * i + rows, total, 0.0), axis=1, keepdims=True)
        for i in range(4)
    )
    alpha = rr_old / curv
    rr_new = rr_old - alpha * (2.0 * res_image - alpha * image_sq)
    direction = dir_ref[...]
    residual = res_ref[...] - alpha * image_ref[...]
    new_sol[...] = sol_ref[...] + alpha * direction
    new_res[...] = residual
    new_dir[...] = residual + (rr_new / rr_old) * direction


def call(kernel, outs, *args, smem=0, scratch=(), limit=16 << 20, cost=None):
    vmem, scalars = pl.BlockSpec(memory_space=pltpu.VMEM), pl.BlockSpec(memory_space=pltpu.SMEM)
    many = isinstance(outs, list)
    return pl.pallas_call(
        kernel,
        out_shape=outs,
        in_specs=[scalars if i < smem else vmem for i in range(len(args))],
        out_specs=[vmem] * len(outs) if many else vmem,
        scratch_shapes=scratch,
        cost_estimate=cost,
        compiler_params=pltpu.CompilerParams(vmem_limit_bytes=limit),
    )(*args)


def shards(points, lengthscale, outputscale, noise, solution, residual, direction):
    def array(*shape, dtype=f32):
        return jax.ShapeDtypeStruct(shape, dtype)

    def partner(group, col):
        return (group + (col if col else groups // 2)) % groups

    def send_body(len_ref, pts_ref, dir_ref, out_ref):
        send_kernel(pts_ref, len_ref, dir_ref, out_ref)

    sent = call(
        send_body, array(per_group, 16, width), lengthscale, points, direction, smem=1
    )
    own = lax.all_to_all(sent, "col", split_axis=0, concat_axis=0)
    places = [(group, col) for group in range(groups) for col in range(per_group)]
    fetch = [
        (partner(group, col) * per_group + col, group * per_group + col) for group, col in places
    ]
    other = lax.ppermute(own, both, fetch)
    left, own_right, own_dir = call(
        own_kernel,
        [
            array(group_pts, depth, dtype=bf16),
            array(depth, group_pts, dtype=bf16),
            array(16, group_pts, dtype=bf16),
        ],
        own,
    )
    place = jnp.stack([lax.axis_index("row"), lax.axis_index("col")]).astype(jnp.int32)
    tile = pltpu.VMEM((width, width), bf16)
    own_out, other_out = call(
        pair_kernel,
        [array(per_group, 8, width), array(per_group, 8, width)],
        place, left, own_right, own_dir, other,
        smem=1,
        scratch=[
            pltpu.VMEM((depth, 2 * group_pts), bf16),
            pltpu.VMEM((16, 2 * group_pts), bf16),
            pltpu.VMEM((16, 2 * group_pts), f32),
            tile, tile, tile, tile,
        ],
        limit=32 << 20,
    )
    back = lax.ppermute(other_out, both, [(to, source) for source, to in fetch])
    parts = lax.all_to_all(own_out + back, "col", split_axis=0, concat_axis=0)
    image, sums = call(
        image_kernel,
        [array(8, width), array(groups * per_group, 128)],
        outputscale, noise, parts, direction, residual,
        smem=2,
    )
    sums = lax.all_to_all(sums, both, split_axis=0, concat_axis=0, tiled=True)
    return tuple(
        call(
            update_kernel,
            [array(8, width)] * 3,
            sums, image, solution, residual, direction,
        )
    )


def solution(mesh):
    spread = P(None, both)
    return jax.shard_map(
        shards,
        mesh=mesh,
        in_specs=(spread, P(), P(), P(), spread, spread, spread),
        out_specs=(spread, spread, spread),
        check_vma=False,
    )
```

```python
import jax
import jax.numpy as jnp
from jax import lax
from jax.experimental import pallas as pl
from jax.experimental.pallas import tpu as pltpu
from jax.sharding import PartitionSpec as P

width = 512
per_group = 8
groups = 16
group_pts = width * per_group
depth = 64
chunk = 128
steps = 65
pts_scale = 5.0**0.5 / 3.0
f32, bf16 = jnp.float32, jnp.bfloat16
nt_dims = (((1,), (1,)), ((), ()))
both = ("row", "col")


def dot(left, right):
    return jnp.dot(left, right, preferred_element_type=f32)


def split(value, parts):
    out = []
    for _ in range(parts):
        top = value.astype(bf16).astype(f32)
        out.append(top)
        value = value - top
    return out


def send_kernel(pts_hbm, len_hbm, dir_hbm, out_ref, pts_ref, len_ref, dir_ref, sems):
    pairs = ((pts_hbm, pts_ref), (len_hbm, len_ref), (dir_hbm, dir_ref))
    copies = [pltpu.make_async_copy(*pair, sems.at[i]) for i, pair in enumerate(pairs)]
    for copy in copies:
        copy.start()
    for copy in copies:
        copy.wait()
    scaled = pts_ref[...] / lengths_of(len_ref) * pts_scale
    direction = dir_ref[...]
    for block in range(per_group):
        out_ref[block, 0:8, :] = scaled
        out_ref[block, 8:16, :] = direction


def lengths_of(len_ref):
    rows = lax.broadcasted_iota(jnp.int32, (8, width), 0)
    lengths = jnp.zeros((8, width), f32)
    for feat in range(8):
        lengths = jnp.where(rows == feat, len_ref[feat], lengths)
    return lengths


def add_kernel(one_ref, two_ref, out_ref):
    out_ref[...] = one_ref[...] + two_ref[...]


def norm_rows(pts, first):
    rows = lax.broadcasted_iota(jnp.int32, pts.shape, 0)
    out = jnp.where(rows < 6, 1.0, 0.0)
    for i, part in enumerate(split(jnp.sum(pts * pts, axis=0, keepdims=True), 3)):
        out = jnp.where(rows == first + i, part, out)
    return out


def right_rows(pts):
    one, two, three = split(pts, 3)
    return jnp.concatenate(
        [one, two, one, three, two, one, norm_rows(pts, 3), jnp.zeros_like(pts)], axis=0
    )


def left_rows(pts):
    one, two, three = split(pts * -2.0, 3)
    return jnp.concatenate(
        [one, one, two, one, two, three, norm_rows(pts, 0), jnp.zeros_like(pts)], axis=0
    )


def right_and_dir(pts, direction, right_ref, dir_ref, at):
    cols = slice(at * width, (at + 1) * width)
    right_ref[:, cols] = right_rows(pts).astype(bf16)
    dir_ref[:, cols] = jnp.concatenate(split(direction, 2), axis=0).astype(bf16)


def own_kernel(own_ref, left_ref, right_ref, dir_ref):
    for at in range(per_group):
        pts = own_ref[at, 0:8, :]
        left_ref[at * width : (at + 1) * width, :] = left_rows(pts).T.astype(bf16)
        right_and_dir(pts, own_ref[at, 8:16, :], right_ref, dir_ref, at)


def matern(dist):
    dist = jnp.maximum(dist, 1e-30)
    radius = dist * lax.rsqrt(dist)
    decay = jnp.exp2(radius * (-3.0 / 0.6931471805599453))
    return ((dist + 1.0 / 3.0) + radius) * decay


def tile_of(step, group, col):
    pair_row, pair_col = step // 8, 8 + step % 8
    last = step == 64
    diag = jnp.where(col <= 3, 4 + col, 0)
    pair_weight = jnp.where(last, jnp.where(col <= 3, 0.5, 0.0), 1.0)
    pair_row, pair_col = jnp.where(last, diag, pair_row), jnp.where(last, diag, pair_col)
    half_row = step // 4
    half_col = 8 + 2 * (step % 4) + (half_row + group // 8) % 2
    inner = step - 32
    shift = 1 + inner // 8
    on_diag = inner >= 28
    inner_row = jnp.where(on_diag, inner - 28, inner % 8)
    inner_col = jnp.where(on_diag, inner_row, (inner_row + shift) % 8)
    first = step < 32
    own_row = jnp.where(first, half_row, inner_row)
    own_col = jnp.where(first, half_col, inner_col)
    own_weight = jnp.where(on_diag, 0.5, 1.0)
    own = col == 0
    return (
        jnp.where(own, own_row, pair_row),
        jnp.where(own, own_col, pair_col),
        jnp.where(own, own_weight, pair_weight),
    )


def pair_kernel(place_ref, left_ref, own_right_ref, own_dir_ref, other_ref, own_out, other_out,
                right_ref, dir_ref, acc_ref, top_even, low_even, top_odd, low_odd):
    group, col = place_ref[0], place_ref[1]
    right_ref[:, :group_pts] = own_right_ref[...]
    dir_ref[:, :group_pts] = own_dir_ref[...]
    for at in range(per_group):
        right_and_dir(other_ref[at, 0:8, :], other_ref[at, 8:16, :], right_ref, dir_ref, per_group + at)
    acc_ref[...] = jnp.zeros_like(acc_ref)

    def evaluate(step, top, low):
        row, column, _ = tile_of(step, group, col)
        row, column = pl.multiple_of(row * width, width), pl.multiple_of(column * width, width)

        def part(at):
            rows = slice(at * chunk, (at + 1) * chunk)
            tile = matern(
                dot(left_ref[pl.ds(row + at * chunk, chunk), :], right_ref[:, pl.ds(column, width)])
            )
            high = tile.astype(bf16)
            top[rows, :] = high
            low[rows, :] = (tile - high.astype(f32)).astype(bf16)

        return [lambda at=at: part(at) for at in range(width // chunk)]

    def multiply(step, top, low):
        row, column, weight = tile_of(step, group, col)
        row, column = pl.multiple_of(row * width, width), pl.multiple_of(column * width, width)

        def to_column(tile):
            acc_ref[:, pl.ds(column, width)] += weight * dot(
                dir_ref[:, pl.ds(row, width)], tile[...]
            )

        def to_row(tile):
            acc_ref[:, pl.ds(row, width)] += weight * lax.dot_general(
                dir_ref[:, pl.ds(column, width)], tile[...], nt_dims, preferred_element_type=f32
            )

        return [
            lambda: to_row(top), lambda: to_column(top), lambda: to_row(low), lambda: to_column(low)
        ]

    def run(first, second):
        for one, two in zip(first, second, strict=True):
            one()
            two()

    for part in evaluate(0, top_even, low_even):
        part()

    def turn(index, carry):
        step = 2 * index
        run(evaluate(step + 1, top_odd, low_odd), multiply(step, top_even, low_even))
        run(evaluate(step + 2, top_even, low_even), multiply(step + 1, top_odd, low_odd))
        return carry

    lax.fori_loop(0, steps // 2, turn, 0, unroll=4)
    for part in multiply(steps - 1, top_even, low_even):
        part()
    for at in range(per_group):
        cols = slice(at * width, (at + 1) * width)
        own_out[at] = acc_ref[0:8, cols] + acc_ref[8:16, cols]
        cols = slice(group_pts + at * width, group_pts + (at + 1) * width)
        other_out[at] = acc_ref[0:8, cols] + acc_ref[8:16, cols]


def image_kernel(scale_ref, noise_ref, parts_ref, dir_ref, res_ref, image_ref, sums_ref):
    product = parts_ref[0]
    for at in range(1, per_group):
        product = product + parts_ref[at]
    direction, residual = dir_ref[...], res_ref[...]
    image = (3.0 * scale_ref[0]) * product + noise_ref[0] * direction
    image_ref[...] = image
    rows = lax.broadcasted_iota(jnp.int32, (8, 128), 0)
    lanes = lax.broadcasted_iota(jnp.int32, (8, 128), 1)
    packed = jnp.zeros((8, 128), f32)
    pairs = ((residual, residual), (direction, image), (residual, image), (image, image))
    for i, (one, two) in enumerate(pairs):
        packed = jnp.where(lanes == 8 * i + rows, jnp.sum(one * two, axis=1, keepdims=True), packed)
    sums_ref[...] = jnp.broadcast_to(jnp.sum(packed, axis=0, keepdims=True), sums_ref.shape)


def update_kernel(sums_ref, image_ref, sol_ref, res_ref, dir_ref, new_sol, new_res, new_dir):
    total = jnp.sum(sums_ref[...], axis=0, keepdims=True)
    rows = lax.broadcasted_iota(jnp.int32, (8, 128), 0)
    lanes = lax.broadcasted_iota(jnp.int32, (8, 128), 1)
    rr_old, curv, res_image, image_sq = (
        jnp.sum(jnp.where(lanes == 8 * i + rows, total, 0.0), axis=1, keepdims=True)
        for i in range(4)
    )
    alpha = rr_old / curv
    rr_new = rr_old - alpha * (2.0 * res_image - alpha * image_sq)
    direction = dir_ref[...]
    residual = res_ref[...] - alpha * image_ref[...]
    new_sol[...] = sol_ref[...] + alpha * direction
    new_res[...] = residual
    new_dir[...] = residual + (rr_new / rr_old) * direction


def call(kernel, outs, *args, smem=0, scratch=(), limit=16 << 20, cost=None):
    vmem, scalars = pl.BlockSpec(memory_space=pltpu.VMEM), pl.BlockSpec(memory_space=pltpu.SMEM)
    many = isinstance(outs, list)
    return pl.pallas_call(
        kernel,
        out_shape=outs,
        in_specs=[scalars if i < smem else vmem for i in range(len(args))],
        out_specs=[vmem] * len(outs) if many else vmem,
        scratch_shapes=scratch,
        cost_estimate=cost,
        compiler_params=pltpu.CompilerParams(vmem_limit_bytes=limit),
    )(*args)


def shards(points, lengthscale, outputscale, noise, solution, residual, direction):
    def array(*shape, dtype=f32):
        return jax.ShapeDtypeStruct(shape, dtype)

    def partner(group, col):
        return (group + (col if col else groups // 2)) % groups

    sent = pl.pallas_call(
        send_kernel,
        out_shape=array(per_group, 16, width),
        in_specs=[pl.BlockSpec(memory_space=pltpu.HBM)] * 3,
        out_specs=pl.BlockSpec(memory_space=pltpu.VMEM),
        scratch_shapes=[
            pltpu.VMEM((8, width), f32),
            pltpu.SMEM((8,), f32),
            pltpu.VMEM((8, width), f32),
            pltpu.SemaphoreType.DMA((3,)),
        ],
        compiler_params=pltpu.CompilerParams(vmem_limit_bytes=62 << 20),
    )(points, lengthscale, direction)
    own = lax.all_to_all(sent, "col", split_axis=0, concat_axis=0)
    places = [(group, col) for group in range(groups) for col in range(per_group)]
    fetch = [
        (partner(group, col) * per_group + col, group * per_group + col) for group, col in places
    ]
    other = lax.ppermute(own, both, fetch)
    left, own_right, own_dir = call(
        own_kernel,
        [
            array(group_pts, depth, dtype=bf16),
            array(depth, group_pts, dtype=bf16),
            array(16, group_pts, dtype=bf16),
        ],
        own,
    )
    place = jnp.stack([lax.axis_index("row"), lax.axis_index("col")]).astype(jnp.int32)
    tile = pltpu.VMEM((width, width), bf16)
    own_out, other_out = call(
        pair_kernel,
        [array(per_group, 8, width), array(per_group, 8, width)],
        place, left, own_right, own_dir, other,
        smem=1,
        scratch=[
            pltpu.VMEM((depth, 2 * group_pts), bf16),
            pltpu.VMEM((16, 2 * group_pts), bf16),
            pltpu.VMEM((16, 2 * group_pts), f32),
            tile, tile, tile, tile,
        ],
        limit=32 << 20,
    )
    back = lax.ppermute(other_out, both, [(to, source) for source, to in fetch])
    total = call(add_kernel, array(per_group, 8, width), own_out, back)
    parts = lax.all_to_all(total, "col", split_axis=0, concat_axis=0)
    image, sums = call(
        image_kernel,
        [array(8, width), array(groups * per_group, 128)],
        outputscale, noise, parts, direction, residual,
        smem=2,
    )
    sums = lax.all_to_all(sums, both, split_axis=0, concat_axis=0, tiled=True)
    return tuple(
        call(
            update_kernel,
            [array(8, width)] * 3,
            sums, image, solution, residual, direction,
        )
    )


def solution(mesh):
    spread = P(None, both)
    return jax.shard_map(
        shards,
        mesh=mesh,
        in_specs=(spread, P(), P(), P(), spread, spread, spread),
        out_specs=(spread, spread, spread),
        check_vma=False,
    )
```

```python
import jax
import jax.numpy as jnp
from jax import lax
from jax.experimental import pallas as pl
from jax.experimental.pallas import tpu as pltpu
from jax.sharding import PartitionSpec as P

width = 512
per_group = 8
groups = 16
group_pts = width * per_group
depth = 64
chunk = 128
half_col = 4
pts_scale = 5.0**0.5 / 3.0
f32, bf16 = jnp.float32, jnp.bfloat16
nt_dims = (((1,), (1,)), ((), ()))
both = ("row", "col")


def dot(left, right):
    return jnp.dot(left, right, preferred_element_type=f32)


def split(value, parts):
    out = []
    for _ in range(parts):
        top = value.astype(bf16).astype(f32)
        out.append(top)
        value = value - top
    return out


def send_kernel(pts_hbm, len_hbm, dir_hbm, out_ref, pts_ref, len_ref, dir_ref, sems):
    pairs = ((pts_hbm, pts_ref), (len_hbm, len_ref), (dir_hbm, dir_ref))
    copies = [pltpu.make_async_copy(*pair, sems.at[i]) for i, pair in enumerate(pairs)]
    for copy in copies:
        copy.start()
    for copy in copies:
        copy.wait()
    scaled = pts_ref[...] / lengths_of(len_ref) * pts_scale
    direction = dir_ref[...]
    for block in range(per_group):
        out_ref[block, 0:8, :] = scaled
        out_ref[block, 8:16, :] = direction


def lengths_of(len_ref):
    rows = lax.broadcasted_iota(jnp.int32, (8, width), 0)
    lengths = jnp.zeros((8, width), f32)
    for feat in range(8):
        lengths = jnp.where(rows == feat, len_ref[feat], lengths)
    return lengths


def add_kernel(one_ref, two_ref, out_ref):
    out_ref[...] = one_ref[...] + two_ref[...]


def norm_rows(pts, first):
    rows = lax.broadcasted_iota(jnp.int32, pts.shape, 0)
    out = jnp.where(rows < 6, 1.0, 0.0)
    for i, part in enumerate(split(jnp.sum(pts * pts, axis=0, keepdims=True), 3)):
        out = jnp.where(rows == first + i, part, out)
    return out


def right_rows(pts):
    one, two, three = split(pts, 3)
    return jnp.concatenate(
        [one, two, one, three, two, one, norm_rows(pts, 3), jnp.zeros_like(pts)], axis=0
    )


def left_rows(pts):
    one, two, three = split(pts * -2.0, 3)
    return jnp.concatenate(
        [one, one, two, one, two, three, norm_rows(pts, 0), jnp.zeros_like(pts)], axis=0
    )


def right_and_dir(pts, direction, right_ref, dir_ref, at):
    cols = slice(at * width, (at + 1) * width)
    right_ref[:, cols] = right_rows(pts).astype(bf16)
    dir_ref[:, cols] = jnp.concatenate(split(direction, 2), axis=0).astype(bf16)


def own_kernel(scale_ref, noise_ref, own_ref, left_ref, right_ref, dir_ref, factor_ref):
    rows = lax.broadcasted_iota(jnp.int32, factor_ref.shape, 0)
    factor_ref[...] = jnp.where(rows == 0, 3.0 * scale_ref[0], noise_ref[0])
    for at in range(per_group):
        pts = own_ref[at, 0:8, :]
        left_ref[at * width : (at + 1) * width, :] = left_rows(pts).T.astype(bf16)
        right_and_dir(pts, own_ref[at, 8:16, :], right_ref, dir_ref, at)


def matern(dist):
    dist = jnp.maximum(dist, 1e-30)
    radius = dist * lax.rsqrt(dist)
    decay = jnp.exp2(radius * (-3.0 / 0.6931471805599453))
    return ((dist + 1.0 / 3.0) + radius) * decay


def tile_of(step, group, col):
    halved = col == half_col
    pairs = jnp.where(halved, 32, 64)
    pair_row = jnp.where(halved, step // 4, step // 8)
    pair_col = 8 + jnp.where(halved, 2 * (step % 4) + (pair_row + group // 8) % 2, step % 8)
    inner = step - pairs + jnp.where(halved, 7, jnp.where(col > half_col, col - 1, col))
    alone = inner >= 28
    row = jnp.where(alone, inner - 28, inner % 8)
    column = jnp.where(alone, row, (row + 1 + inner // 8) % 8)
    mixed = step < pairs
    return (
        jnp.where(mixed, pair_row, row),
        jnp.where(mixed, pair_col, column),
        jnp.where(jnp.logical_and(alone, jnp.logical_not(mixed)), 0.5, 1.0),
    )


def pair_kernel(place_ref, left_ref, own_right_ref, own_dir_ref, other_ref, own_out, other_out,
                right_ref, dir_ref, acc_ref, top_even, low_even, top_odd, low_odd):
    group, col = place_ref[0], place_ref[1]
    right_ref[:, :group_pts] = own_right_ref[...]
    dir_ref[:, :group_pts] = own_dir_ref[...]
    for at in range(per_group):
        right_and_dir(other_ref[at, 0:8, :], other_ref[at, 8:16, :], right_ref, dir_ref, per_group + at)
    acc_ref[...] = jnp.zeros_like(acc_ref)

    def evaluate(step, top, low):
        row, column, _ = tile_of(step, group, col)
        row, column = pl.multiple_of(row * width, width), pl.multiple_of(column * width, width)

        def part(at):
            rows = slice(at * chunk, (at + 1) * chunk)
            tile = matern(
                dot(left_ref[pl.ds(row + at * chunk, chunk), :], right_ref[:, pl.ds(column, width)])
            )
            high = tile.astype(bf16)
            top[rows, :] = high
            low[rows, :] = (tile - high.astype(f32)).astype(bf16)

        return [lambda at=at: part(at) for at in range(width // chunk)]

    def multiply(step, top, low):
        row, column, weight = tile_of(step, group, col)
        row, column = pl.multiple_of(row * width, width), pl.multiple_of(column * width, width)

        def to_column(tile):
            acc_ref[:, pl.ds(column, width)] += weight * dot(
                dir_ref[:, pl.ds(row, width)], tile[...]
            )

        def to_row(tile):
            acc_ref[:, pl.ds(row, width)] += weight * lax.dot_general(
                dir_ref[:, pl.ds(column, width)], tile[...], nt_dims, preferred_element_type=f32
            )

        return [
            lambda: to_row(top), lambda: to_column(top), lambda: to_row(low), lambda: to_column(low)
        ]

    def run(first, second):
        for one, two in zip(first, second, strict=True):
            one()
            two()

    for part in evaluate(0, top_even, low_even):
        part()

    def turn(index, carry):
        step = 2 * index
        run(evaluate(step + 1, top_odd, low_odd), multiply(step, top_even, low_even))
        run(evaluate(step + 2, top_even, low_even), multiply(step + 1, top_odd, low_odd))
        return carry

    lax.fori_loop(0, 28, turn, 0, unroll=4)
    halved = col == half_col

    def last_turns(index, carry):
        return turn(2 * index + 29, turn(2 * index + 28, carry))

    lax.fori_loop(0, jnp.where(halved, 1, 2), last_turns, 0)
    for part in multiply(jnp.where(halved, 60, 64), top_even, low_even):
        part()
    for at in range(per_group):
        cols = slice(at * width, (at + 1) * width)
        own_out[at] = acc_ref[0:8, cols] + acc_ref[8:16, cols]
        cols = slice(group_pts + at * width, group_pts + (at + 1) * width)
        other_out[at] = acc_ref[0:8, cols] + acc_ref[8:16, cols]


def image_kernel(factor_ref, parts_ref, dir_ref, res_ref, image_ref, sums_ref):
    product = parts_ref[0]
    for at in range(1, per_group):
        product = product + parts_ref[at]
    direction, residual = dir_ref[...], res_ref[...]
    image = factor_ref[0:1, 0:1] * product + factor_ref[1:2, 0:1] * direction
    image_ref[...] = image
    rows = lax.broadcasted_iota(jnp.int32, (8, 128), 0)
    lanes = lax.broadcasted_iota(jnp.int32, (8, 128), 1)
    packed = jnp.zeros((8, 128), f32)
    pairs = ((residual, residual), (direction, image), (residual, image), (image, image))
    for i, (one, two) in enumerate(pairs):
        packed = jnp.where(lanes == 8 * i + rows, jnp.sum(one * two, axis=1, keepdims=True), packed)
    sums_ref[...] = jnp.broadcast_to(jnp.sum(packed, axis=0, keepdims=True), sums_ref.shape)


def update_kernel(sums_ref, image_ref, sol_ref, res_ref, dir_ref, new_sol, new_res, new_dir):
    total = jnp.sum(sums_ref[...], axis=0, keepdims=True)
    rows = lax.broadcasted_iota(jnp.int32, (8, 128), 0)
    lanes = lax.broadcasted_iota(jnp.int32, (8, 128), 1)
    rr_old, curv, res_image, image_sq = (
        jnp.sum(jnp.where(lanes == 8 * i + rows, total, 0.0), axis=1, keepdims=True)
        for i in range(4)
    )
    alpha = rr_old / curv
    rr_new = rr_old - alpha * (2.0 * res_image - alpha * image_sq)
    direction = dir_ref[...]
    residual = res_ref[...] - alpha * image_ref[...]
    new_sol[...] = sol_ref[...] + alpha * direction
    new_res[...] = residual
    new_dir[...] = residual + (rr_new / rr_old) * direction


def call(kernel, outs, *args, smem=0, scratch=(), limit=16 << 20, cost=None):
    vmem, scalars = pl.BlockSpec(memory_space=pltpu.VMEM), pl.BlockSpec(memory_space=pltpu.SMEM)
    many = isinstance(outs, list)
    return pl.pallas_call(
        kernel,
        out_shape=outs,
        in_specs=[scalars if i < smem else vmem for i in range(len(args))],
        out_specs=[vmem] * len(outs) if many else vmem,
        scratch_shapes=scratch,
        cost_estimate=cost,
        compiler_params=pltpu.CompilerParams(vmem_limit_bytes=limit),
    )(*args)


def shards(points, lengthscale, outputscale, noise, solution, residual, direction):
    def array(*shape, dtype=f32):
        return jax.ShapeDtypeStruct(shape, dtype)

    def partner(group, col):
        z, x = divmod(group, 4)
        if col == 1:
            dz, dx = ((0, 2), (2, 0))[(z // 2 + x // 2 + 1) % 2]
        else:
            dz, dx = {4: (-2, -2), 5: (0, 1), 6: (-1, -2), 7: (1, 0), 2: (-2, -1), 3: (-1, -1), 0: (-1, 1)}[col]
        return (z + dz) % 4 * 4 + (x + dx) % 4

    sent = pl.pallas_call(
        send_kernel,
        out_shape=array(per_group, 16, width),
        in_specs=[pl.BlockSpec(memory_space=pltpu.HBM)] * 3,
        out_specs=pl.BlockSpec(memory_space=pltpu.VMEM),
        scratch_shapes=[
            pltpu.VMEM((8, width), f32),
            pltpu.SMEM((8,), f32),
            pltpu.VMEM((8, width), f32),
            pltpu.SemaphoreType.DMA((3,)),
        ],
        compiler_params=pltpu.CompilerParams(vmem_limit_bytes=62 << 20),
    )(points, lengthscale, direction)
    own = lax.all_to_all(sent, "col", split_axis=0, concat_axis=0)
    places = [(group, col) for group in range(groups) for col in range(per_group)]
    fetch = [
        (partner(group, col) * per_group + col, group * per_group + col) for group, col in places
    ]
    other = lax.ppermute(own, both, fetch)
    left, own_right, own_dir, factors = call(
        own_kernel,
        [
            array(group_pts, depth, dtype=bf16),
            array(depth, group_pts, dtype=bf16),
            array(16, group_pts, dtype=bf16),
            array(8, 128),
        ],
        outputscale, noise, own,
        smem=2,
    )
    place = jnp.stack([lax.axis_index("row"), lax.axis_index("col")]).astype(jnp.int32)
    tile = pltpu.VMEM((width, width), bf16)
    own_out, other_out = call(
        pair_kernel,
        [array(per_group, 8, width), array(per_group, 8, width)],
        place, left, own_right, own_dir, other,
        smem=1,
        scratch=[
            pltpu.VMEM((depth, 2 * group_pts), bf16),
            pltpu.VMEM((16, 2 * group_pts), bf16),
            pltpu.VMEM((16, 2 * group_pts), f32),
            tile, tile, tile, tile,
        ],
        limit=32 << 20,
    )
    back = lax.ppermute(other_out, both, [(to, source) for source, to in fetch])
    total = call(add_kernel, array(per_group, 8, width), own_out, back)
    parts = lax.all_to_all(total, "col", split_axis=0, concat_axis=0)
    image, sums = call(
        image_kernel,
        [array(8, width), array(groups * per_group, 128)],
        factors, parts, direction, residual,
    )
    sums = lax.all_to_all(sums, both, split_axis=0, concat_axis=0, tiled=True)
    return tuple(
        call(
            update_kernel,
            [array(8, width)] * 3,
            sums, image, solution, residual, direction,
        )
    )


def solution(mesh):
    spread = P(None, both)
    return jax.shard_map(
        shards,
        mesh=mesh,
        in_specs=(spread, P(), P(), P(), spread, spread, spread),
        out_specs=(spread, spread, spread),
        check_vma=False,
    )
```

```python
import jax
import jax.numpy as jnp
from jax import lax
from jax.experimental import pallas as pl
from jax.experimental.pallas import tpu as pltpu
from jax.sharding import PartitionSpec as P

width = 512
per_group = 8
groups = 16
early = 2
group_pts = width * per_group
depth = 64
chunk = 128
half_col = 4
pts_scale = 5.0**0.5 / 3.0
f32, bf16 = jnp.float32, jnp.bfloat16
nt_dims = (((1,), (1,)), ((), ()))
both = ("row", "col")


def dot(left, right):
    return jnp.dot(left, right, preferred_element_type=f32)


def split(value, parts):
    out = []
    for _ in range(parts):
        top = value.astype(bf16).astype(f32)
        out.append(top)
        value = value - top
    return out


def send_kernel(pts_hbm, len_hbm, dir_hbm, out_ref, pts_ref, len_ref, dir_ref, sems):
    pairs = ((pts_hbm, pts_ref), (len_hbm, len_ref), (dir_hbm, dir_ref))
    copies = [pltpu.make_async_copy(*pair, sems.at[i]) for i, pair in enumerate(pairs)]
    for copy in copies:
        copy.start()
    for copy in copies:
        copy.wait()
    scaled = pts_ref[...] / lengths_of(len_ref) * pts_scale
    direction = dir_ref[...]
    for block in range(per_group):
        out_ref[block, 0:8, :] = scaled
        out_ref[block, 8:16, :] = direction


def lengths_of(len_ref):
    rows = lax.broadcasted_iota(jnp.int32, (8, width), 0)
    lengths = jnp.zeros((8, width), f32)
    for feat in range(8):
        lengths = jnp.where(rows == feat, len_ref[feat], lengths)
    return lengths


def add_kernel(one_ref, two_ref, out_ref):
    out_ref[...] = one_ref[...] + two_ref[...]


def norm_rows(pts, first):
    rows = lax.broadcasted_iota(jnp.int32, pts.shape, 0)
    out = jnp.where(rows < 6, 1.0, 0.0)
    for i, part in enumerate(split(jnp.sum(pts * pts, axis=0, keepdims=True), 3)):
        out = jnp.where(rows == first + i, part, out)
    return out


def right_rows(pts):
    one, two, three = split(pts, 3)
    return jnp.concatenate(
        [one, two, one, three, two, one, norm_rows(pts, 3), jnp.zeros_like(pts)], axis=0
    )


def left_rows(pts):
    one, two, three = split(pts * -2.0, 3)
    return jnp.concatenate(
        [one, one, two, one, two, three, norm_rows(pts, 0), jnp.zeros_like(pts)], axis=0
    )


def right_and_dir(pts, direction, right_ref, dir_ref, at):
    cols = slice(at * width, (at + 1) * width)
    right_ref[:, cols] = right_rows(pts).astype(bf16)
    dir_ref[:, cols] = jnp.concatenate(split(direction, 2), axis=0).astype(bf16)


def own_kernel(scale_ref, noise_ref, own_ref, left_ref, right_ref, dir_ref, factor_ref):
    rows = lax.broadcasted_iota(jnp.int32, factor_ref.shape, 0)
    factor_ref[...] = jnp.where(rows == 0, 3.0 * scale_ref[0], noise_ref[0])
    for at in range(per_group):
        pts = own_ref[at, 0:8, :]
        left_ref[at * width : (at + 1) * width, :] = left_rows(pts).T.astype(bf16)
        right_and_dir(pts, own_ref[at, 8:16, :], right_ref, dir_ref, at)


def matern(dist):
    dist = jnp.maximum(dist, 1e-30)
    radius = dist * lax.rsqrt(dist)
    decay = jnp.exp2(radius * (-3.0 / 0.6931471805599453))
    return ((dist + 1.0 / 3.0) + radius) * decay


def tile_of(step, group, col, blocks, alone_from, inner_from):
    halved = col == half_col
    pairs = jnp.where(halved, 4 * blocks, 8 * blocks)
    pair_row = step % 8
    pair_col = 8 + jnp.where(halved, 2 * (step // 8) + (pair_row + group // 8) % 2, step // 8)
    inner = step - pairs + jnp.where(halved, inner_from, jnp.where(col > half_col, col - 1, col))
    alone = inner >= alone_from
    row = jnp.where(alone, inner - alone_from, inner % 8)
    column = jnp.where(alone, row, (row + 1 + inner // 8) % 8)
    mixed = step < pairs
    return (
        jnp.where(mixed, pair_row, row),
        jnp.where(mixed, pair_col, column),
        jnp.where(jnp.logical_and(alone, jnp.logical_not(mixed)), 0.5, 1.0),
    )


def pair_kernel(blocks, inner_from, turns, place_ref, left_ref, own_right_ref, own_dir_ref, other_ref, *refs):
    before_ref = None
    if len(refs) == 11:
        before_ref, first_ref, *refs = refs
    own_out, other_out, right_ref, dir_ref, acc_ref, top_even, low_even, top_odd, low_odd = refs
    group, col = place_ref[0], place_ref[1]
    halved = col == half_col
    right_ref[:, :group_pts] = own_right_ref[...]
    dir_ref[:, :group_pts] = own_dir_ref[...]
    for at in range(blocks):
        right_and_dir(other_ref[at, 0:8, :], other_ref[at, 8:16, :], right_ref, dir_ref, per_group + at)
    acc_ref[...] = jnp.zeros_like(acc_ref)
    if before_ref is not None:
        for at in range(per_group):
            acc_ref[0:8, at * width : (at + 1) * width] = before_ref[at]

    def place_of(step):
        row, column, weight = tile_of(step, group, col, blocks, 28, inner_from)
        return pl.multiple_of(row * width, width), pl.multiple_of(column * width, width), weight

    def evaluate(step, top, low):
        row, column, _ = place_of(step)

        def part(at):
            rows = slice(at * chunk, (at + 1) * chunk)
            tile = matern(
                dot(left_ref[pl.ds(row + at * chunk, chunk), :], right_ref[:, pl.ds(column, width)])
            )
            high = tile.astype(bf16)
            top[rows, :] = high
            low[rows, :] = (tile - high.astype(f32)).astype(bf16)

        return [lambda at=at: part(at) for at in range(width // chunk)]

    def multiply(step, top, low):
        row, column, weight = place_of(step)

        def to_column(tile):
            acc_ref[:, pl.ds(column, width)] += weight * dot(
                dir_ref[:, pl.ds(row, width)], tile[...]
            )

        def to_row(tile):
            acc_ref[:, pl.ds(row, width)] += weight * lax.dot_general(
                dir_ref[:, pl.ds(column, width)], tile[...], nt_dims, preferred_element_type=f32
            )

        return [
            lambda: to_row(top), lambda: to_column(top), lambda: to_row(low), lambda: to_column(low)
        ]

    def run(first, second):
        for one, two in zip(first, second, strict=True):
            one()
            two()

    for part in evaluate(0, top_even, low_even):
        part()

    def turn(index, carry):
        step = 2 * index
        run(evaluate(step + 1, top_odd, low_odd), multiply(step, top_even, low_even))
        run(evaluate(step + 2, top_even, low_even), multiply(step + 1, top_odd, low_odd))
        return carry

    turns(halved, turn, evaluate, multiply, run, (top_even, low_even), (top_odd, low_odd))
    for at in range(per_group):
        cols = slice(at * width, (at + 1) * width)
        own_out[at] = acc_ref[0:8, cols] + acc_ref[8:16, cols]
    if before_ref is not None:
        other_out[0:early] = first_ref[...]
    for at in range(blocks):
        cols = slice(group_pts + at * width, group_pts + (at + 1) * width)
        other_out[at + other_out.shape[0] - blocks] = acc_ref[0:8, cols] + acc_ref[8:16, cols]


def first_turns(halved, turn, evaluate, multiply, run, even, odd):
    lax.fori_loop(0, 6, turn, 0, unroll=3)
    turn(6, 0)
    run(evaluate(15, *odd), multiply(14, *even))
    for part in multiply(15, *odd):
        part()


def later_turns(halved, turn, evaluate, multiply, run, even, odd):
    lax.fori_loop(0, 20, turn, 0, unroll=4)

    def last_turns(index, carry):
        return turn(2 * index + 21, turn(2 * index + 20, carry))

    lax.fori_loop(0, jnp.where(halved, 1, 2), last_turns, 0)
    for part in multiply(jnp.where(halved, 44, 48), *even):
        part()


def image_kernel(factor_ref, parts_ref, dir_ref, res_ref, image_ref, sums_ref):
    product = parts_ref[0]
    for at in range(1, per_group):
        product = product + parts_ref[at]
    direction, residual = dir_ref[...], res_ref[...]
    image = factor_ref[0:1, 0:1] * product + factor_ref[1:2, 0:1] * direction
    image_ref[...] = image
    rows = lax.broadcasted_iota(jnp.int32, (8, 128), 0)
    lanes = lax.broadcasted_iota(jnp.int32, (8, 128), 1)
    packed = jnp.zeros((8, 128), f32)
    pairs = ((residual, residual), (direction, image), (residual, image), (image, image))
    for i, (one, two) in enumerate(pairs):
        packed = jnp.where(lanes == 8 * i + rows, jnp.sum(one * two, axis=1, keepdims=True), packed)
    sums_ref[...] = jnp.broadcast_to(jnp.sum(packed, axis=0, keepdims=True), sums_ref.shape)


def update_kernel(sums_ref, image_ref, sol_ref, res_ref, dir_ref, new_sol, new_res, new_dir):
    total = jnp.sum(sums_ref[...], axis=0, keepdims=True)
    rows = lax.broadcasted_iota(jnp.int32, (8, 128), 0)
    lanes = lax.broadcasted_iota(jnp.int32, (8, 128), 1)
    rr_old, curv, res_image, image_sq = (
        jnp.sum(jnp.where(lanes == 8 * i + rows, total, 0.0), axis=1, keepdims=True)
        for i in range(4)
    )
    alpha = rr_old / curv
    rr_new = rr_old - alpha * (2.0 * res_image - alpha * image_sq)
    direction = dir_ref[...]
    residual = res_ref[...] - alpha * image_ref[...]
    new_sol[...] = sol_ref[...] + alpha * direction
    new_res[...] = residual
    new_dir[...] = residual + (rr_new / rr_old) * direction


def call(kernel, outs, *args, smem=0, scratch=(), limit=16 << 20, cost=None):
    vmem, scalars = pl.BlockSpec(memory_space=pltpu.VMEM), pl.BlockSpec(memory_space=pltpu.SMEM)
    many = isinstance(outs, list)
    return pl.pallas_call(
        kernel,
        out_shape=outs,
        in_specs=[scalars if i < smem else vmem for i in range(len(args))],
        out_specs=[vmem] * len(outs) if many else vmem,
        scratch_shapes=scratch,
        cost_estimate=cost,
        compiler_params=pltpu.CompilerParams(vmem_limit_bytes=limit),
    )(*args)


def shards(points, lengthscale, outputscale, noise, solution, residual, direction):
    def array(*shape, dtype=f32):
        return jax.ShapeDtypeStruct(shape, dtype)

    def partner(group, col):
        z, x = divmod(group, 4)
        if col == 1:
            dz, dx = ((0, 2), (2, 0))[(z // 2 + x // 2 + 1) % 2]
        else:
            dz, dx = {4: (-2, -2), 5: (0, 1), 6: (-1, -2), 7: (1, 0), 2: (-2, -1), 3: (-1, -1), 0: (-1, 1)}[col]
        return (z + dz) % 4 * 4 + (x + dx) % 4

    sent = pl.pallas_call(
        send_kernel,
        out_shape=array(per_group, 16, width),
        in_specs=[pl.BlockSpec(memory_space=pltpu.HBM)] * 3,
        out_specs=pl.BlockSpec(memory_space=pltpu.VMEM),
        scratch_shapes=[
            pltpu.VMEM((8, width), f32),
            pltpu.SMEM((8,), f32),
            pltpu.VMEM((8, width), f32),
            pltpu.SemaphoreType.DMA((3,)),
        ],
        compiler_params=pltpu.CompilerParams(vmem_limit_bytes=62 << 20),
    )(points, lengthscale, direction)
    own = lax.all_to_all(sent, "col", split_axis=0, concat_axis=0)
    places = [(group, col) for group in range(groups) for col in range(per_group)]
    fetch = [
        (partner(group, col) * per_group + col, group * per_group + col) for group, col in places
    ]
    other_first = lax.ppermute(own[:early], both, fetch)
    other_later = lax.ppermute(own[early:], both, fetch)
    left, own_right, own_dir, factors = call(
        own_kernel,
        [
            array(group_pts, depth, dtype=bf16),
            array(depth, group_pts, dtype=bf16),
            array(16, group_pts, dtype=bf16),
            array(8, 128),
        ],
        outputscale, noise, own,
        smem=2,
    )
    place = jnp.stack([lax.axis_index("row"), lax.axis_index("col")]).astype(jnp.int32)
    tile = pltpu.VMEM((width, width), bf16)

    def pair_call(blocks, inner_from, turns, tiles, *args):
        def body(*refs):
            pair_kernel(blocks, inner_from, turns, *refs)

        pairs = tiles * width * width
        pts = group_pts + blocks * width
        return call(
            body,
            [array(per_group, 8, width), array(per_group if len(args) > 1 else blocks, 8, width)],
            place, left, own_right, own_dir, *args,
            smem=1,
            scratch=[
                pltpu.VMEM((depth, pts), bf16),
                pltpu.VMEM((16, pts), bf16),
                pltpu.VMEM((16, pts), f32),
                tile, tile, tile, tile,
            ],
            limit=32 << 20,
            cost=pl.CostEstimate(
                flops=256 * pairs, transcendentals=2 * pairs, bytes_accessed=1 << 21
            ),
        )

    own_first, out_first = pair_call(early, 7, first_turns, 16, other_first)
    own_all, out_all = pair_call(
        per_group - early, 15, later_turns, 49, other_later, own_first, out_first
    )
    back = lax.ppermute(out_all, both, [(to, source) for source, to in fetch])
    total = call(add_kernel, array(per_group, 8, width), own_all, back)
    parts = lax.all_to_all(total, "col", split_axis=0, concat_axis=0)
    image, sums = call(
        image_kernel,
        [array(8, width), array(groups * per_group, 128)],
        factors, parts, direction, residual,
    )
    sums = lax.all_to_all(sums, both, split_axis=0, concat_axis=0, tiled=True)
    return tuple(
        call(
            update_kernel,
            [array(8, width)] * 3,
            sums, image, solution, residual, direction,
        )
    )


def solution(mesh):
    spread = P(None, both)
    return jax.shard_map(
        shards,
        mesh=mesh,
        in_specs=(spread, P(), P(), P(), spread, spread, spread),
        out_specs=(spread, spread, spread),
        check_vma=False,
    )
```

```python
import jax
import jax.numpy as jnp
from jax import lax
from jax.experimental import pallas as pl
from jax.experimental.pallas import tpu as pltpu
from jax.sharding import PartitionSpec as P

width = 512
per_group = 8
groups = 16
early = 2
group_pts = width * per_group
depth = 64
chunk = 128
half_col = 4
pts_scale = 5.0**0.5 / 3.0
f32, bf16 = jnp.float32, jnp.bfloat16
nt_dims = (((1,), (1,)), ((), ()))
both = ("row", "col")


def dot(left, right):
    return jnp.dot(left, right, preferred_element_type=f32)


def split(value, parts):
    out = []
    for _ in range(parts):
        top = value.astype(bf16).astype(f32)
        out.append(top)
        value = value - top
    return out


def send_kernel(pts_hbm, len_hbm, dir_hbm, out_ref, pts_ref, len_ref, dir_ref, sems):
    pairs = ((pts_hbm, pts_ref), (len_hbm, len_ref), (dir_hbm, dir_ref))
    copies = [pltpu.make_async_copy(*pair, sems.at[i]) for i, pair in enumerate(pairs)]
    for copy in copies:
        copy.start()
    for copy in copies:
        copy.wait()
    scaled = pts_ref[...] / lengths_of(len_ref) * pts_scale
    direction = dir_ref[...]
    for block in range(per_group):
        out_ref[block, 0:8, :] = scaled
        out_ref[block, 8:16, :] = direction


def lengths_of(len_ref):
    rows = lax.broadcasted_iota(jnp.int32, (8, width), 0)
    lengths = jnp.zeros((8, width), f32)
    for feat in range(8):
        lengths = jnp.where(rows == feat, len_ref[feat], lengths)
    return lengths


def add_kernel(one_ref, two_ref, out_ref):
    out_ref[...] = one_ref[...] + two_ref[...]


def norm_rows(pts, first):
    rows = lax.broadcasted_iota(jnp.int32, pts.shape, 0)
    out = jnp.where(rows < 6, 1.0, 0.0)
    for i, part in enumerate(split(jnp.sum(pts * pts, axis=0, keepdims=True), 3)):
        out = jnp.where(rows == first + i, part, out)
    return out


def right_rows(pts):
    one, two, three = split(pts, 3)
    return jnp.concatenate(
        [one, two, one, three, two, one, norm_rows(pts, 3), jnp.zeros_like(pts)], axis=0
    )


def left_rows(pts):
    one, two, three = split(pts * -2.0, 3)
    return jnp.concatenate(
        [one, one, two, one, two, three, norm_rows(pts, 0), jnp.zeros_like(pts)], axis=0
    )


def right_and_dir(pts, direction, right_ref, dir_ref, at):
    cols = slice(at * width, (at + 1) * width)
    right_ref[:, cols] = right_rows(pts).astype(bf16)
    dir_ref[:, cols] = jnp.concatenate(split(direction, 2), axis=0).astype(bf16)


def own_kernel(scale_ref, noise_ref, own_ref, left_ref, right_ref, dir_ref, factor_ref):
    rows = lax.broadcasted_iota(jnp.int32, factor_ref.shape, 0)
    factor_ref[...] = jnp.where(rows == 0, 3.0 * scale_ref[0], noise_ref[0])
    for at in range(per_group):
        pts = own_ref[at, 0:8, :]
        left_ref[at * width : (at + 1) * width, :] = left_rows(pts).T.astype(bf16)
        right_and_dir(pts, own_ref[at, 8:16, :], right_ref, dir_ref, at)


def matern(dist):
    dist = jnp.maximum(dist, 1e-30)
    radius = dist * lax.rsqrt(dist)
    decay = jnp.exp2(radius * (-3.0 / 0.6931471805599453))
    return ((dist + 1.0 / 3.0) + radius) * decay


def tile_of(step, group, col, blocks, alone_from, inner_from):
    halved = col == half_col
    pairs = jnp.where(halved, 4 * blocks, 8 * blocks)
    pair_row = step % 8
    pair_col = 8 + jnp.where(halved, 2 * (step // 8) + (pair_row + group // 8) % 2, step // 8)
    inner = step - pairs + jnp.where(halved, inner_from, jnp.where(col > half_col, col - 1, col))
    alone = inner >= alone_from
    row = jnp.where(alone, inner - alone_from, inner % 8)
    column = jnp.where(alone, row, (row + 1 + inner // 8) % 8)
    mixed = step < pairs
    return (
        jnp.where(mixed, pair_row, row),
        jnp.where(mixed, pair_col, column),
        jnp.where(jnp.logical_and(alone, jnp.logical_not(mixed)), 0.5, 1.0),
    )


def pair_kernel(blocks, inner_from, turns, place_ref, left_ref, own_right_ref, own_dir_ref, other_ref, *refs):
    before_ref = None
    if len(refs) == 13:
        before_ref, first_ref, top_in, low_in, *refs = refs
        own_out, other_out, right_ref, dir_ref, acc_ref, top_odd, low_odd, top_even, low_even = refs
    else:
        own_out, other_out, top_even, low_even, right_ref, dir_ref, acc_ref, top_odd, low_odd = refs
    group, col = place_ref[0], place_ref[1]
    halved = col == half_col
    right_ref[:, :group_pts] = own_right_ref[...]
    dir_ref[:, :group_pts] = own_dir_ref[...]
    for at in range(blocks):
        right_and_dir(other_ref[at, 0:8, :], other_ref[at, 8:16, :], right_ref, dir_ref, per_group + at)
    acc_ref[...] = jnp.zeros_like(acc_ref)
    if before_ref is not None:
        for at in range(per_group):
            acc_ref[0:8, at * width : (at + 1) * width] = before_ref[at]

    def place_of(step):
        if before_ref is None:
            row, column, weight = tile_of(step, group, col, blocks, 28, inner_from)
        else:
            handed = tile_of(16, group, col, early, 28, 7)
            later = tile_of(step - 1, group, col, blocks, 28, inner_from)
            row, column, weight = (
                jnp.where(step == 0, one, two) for one, two in zip(handed, later, strict=True)
            )
        return pl.multiple_of(row * width, width), pl.multiple_of(column * width, width), weight

    def evaluate(step, top, low):
        row, column, _ = place_of(step)

        def part(at):
            rows = slice(at * chunk, (at + 1) * chunk)
            tile = matern(
                dot(left_ref[pl.ds(row + at * chunk, chunk), :], right_ref[:, pl.ds(column, width)])
            )
            high = tile.astype(bf16)
            top[rows, :] = high
            low[rows, :] = (tile - high.astype(f32)).astype(bf16)

        return [lambda at=at: part(at) for at in range(width // chunk)]

    def multiply(step, top, low):
        row, column, weight = place_of(step)

        def to_column(tile):
            acc_ref[:, pl.ds(column, width)] += weight * dot(
                dir_ref[:, pl.ds(row, width)], tile[...]
            )

        def to_row(tile):
            acc_ref[:, pl.ds(row, width)] += weight * lax.dot_general(
                dir_ref[:, pl.ds(column, width)], tile[...], nt_dims, preferred_element_type=f32
            )

        return [
            lambda: to_row(top), lambda: to_column(top), lambda: to_row(low), lambda: to_column(low)
        ]

    def run(first, second):
        for one, two in zip(first, second, strict=True):
            one()
            two()

    if before_ref is None:
        for part in evaluate(0, top_even, low_even):
            part()
    else:
        top_even[...] = top_in[...]
        low_even[...] = low_in[...]

    def turn(index, carry):
        step = 2 * index
        run(evaluate(step + 1, top_odd, low_odd), multiply(step, top_even, low_even))
        run(evaluate(step + 2, top_even, low_even), multiply(step + 1, top_odd, low_odd))
        return carry

    turns(halved, turn, evaluate, multiply, run, (top_even, low_even), (top_odd, low_odd))
    for at in range(per_group):
        cols = slice(at * width, (at + 1) * width)
        own_out[at] = acc_ref[0:8, cols] + acc_ref[8:16, cols]
    if before_ref is not None:
        other_out[0:early] = first_ref[...]
    for at in range(blocks):
        cols = slice(group_pts + at * width, group_pts + (at + 1) * width)
        other_out[at + other_out.shape[0] - blocks] = acc_ref[0:8, cols] + acc_ref[8:16, cols]


def first_turns(halved, turn, evaluate, multiply, run, even, odd):
    lax.fori_loop(0, 8, turn, 0, unroll=4)


def later_turns(halved, turn, evaluate, multiply, run, even, odd):
    lax.fori_loop(0, 20, turn, 0, unroll=4)

    def last_turns(index, carry):
        return turn(2 * index + 21, turn(2 * index + 20, carry))

    lax.fori_loop(0, jnp.where(halved, 1, 2), last_turns, 0)
    for part in multiply(jnp.where(halved, 44, 48), *even):
        part()


def image_kernel(factor_ref, parts_ref, dir_ref, res_ref, image_ref, sums_ref):
    product = parts_ref[0]
    for at in range(1, per_group):
        product = product + parts_ref[at]
    direction, residual = dir_ref[...], res_ref[...]
    image = factor_ref[0:1, 0:1] * product + factor_ref[1:2, 0:1] * direction
    image_ref[...] = image
    rows = lax.broadcasted_iota(jnp.int32, (8, 128), 0)
    lanes = lax.broadcasted_iota(jnp.int32, (8, 128), 1)
    packed = jnp.zeros((8, 128), f32)
    pairs = ((residual, residual), (direction, image), (residual, image), (image, image))
    for i, (one, two) in enumerate(pairs):
        packed = jnp.where(lanes == 8 * i + rows, jnp.sum(one * two, axis=1, keepdims=True), packed)
    sums_ref[...] = jnp.broadcast_to(jnp.sum(packed, axis=0, keepdims=True), sums_ref.shape)


def update_kernel(sums_ref, image_ref, sol_ref, res_ref, dir_ref, new_sol, new_res, new_dir):
    total = jnp.sum(sums_ref[...], axis=0, keepdims=True)
    rows = lax.broadcasted_iota(jnp.int32, (8, 128), 0)
    lanes = lax.broadcasted_iota(jnp.int32, (8, 128), 1)
    rr_old, curv, res_image, image_sq = (
        jnp.sum(jnp.where(lanes == 8 * i + rows, total, 0.0), axis=1, keepdims=True)
        for i in range(4)
    )
    alpha = rr_old / curv
    rr_new = rr_old - alpha * (2.0 * res_image - alpha * image_sq)
    direction = dir_ref[...]
    residual = res_ref[...] - alpha * image_ref[...]
    new_sol[...] = sol_ref[...] + alpha * direction
    new_res[...] = residual
    new_dir[...] = residual + (rr_new / rr_old) * direction


def call(kernel, outs, *args, smem=0, scratch=(), limit=16 << 20, cost=None):
    vmem, scalars = pl.BlockSpec(memory_space=pltpu.VMEM), pl.BlockSpec(memory_space=pltpu.SMEM)
    many = isinstance(outs, list)
    return pl.pallas_call(
        kernel,
        out_shape=outs,
        in_specs=[scalars if i < smem else vmem for i in range(len(args))],
        out_specs=[vmem] * len(outs) if many else vmem,
        scratch_shapes=scratch,
        cost_estimate=cost,
        compiler_params=pltpu.CompilerParams(vmem_limit_bytes=limit),
    )(*args)


def shards(points, lengthscale, outputscale, noise, solution, residual, direction):
    def array(*shape, dtype=f32):
        return jax.ShapeDtypeStruct(shape, dtype)

    def partner(group, col):
        z, x = divmod(group, 4)
        if col == 1:
            dz, dx = ((0, 2), (2, 0))[(z // 2 + x // 2 + 1) % 2]
        else:
            dz, dx = {4: (-2, -2), 5: (0, 1), 6: (-1, -2), 7: (1, 0), 2: (-2, -1), 3: (-1, -1), 0: (-1, 1)}[col]
        return (z + dz) % 4 * 4 + (x + dx) % 4

    sent = pl.pallas_call(
        send_kernel,
        out_shape=array(per_group, 16, width),
        in_specs=[pl.BlockSpec(memory_space=pltpu.HBM)] * 3,
        out_specs=pl.BlockSpec(memory_space=pltpu.VMEM),
        scratch_shapes=[
            pltpu.VMEM((8, width), f32),
            pltpu.SMEM((8,), f32),
            pltpu.VMEM((8, width), f32),
            pltpu.SemaphoreType.DMA((3,)),
        ],
        compiler_params=pltpu.CompilerParams(vmem_limit_bytes=62 << 20),
    )(points, lengthscale, direction)
    own = lax.all_to_all(sent, "col", split_axis=0, concat_axis=0)
    places = [(group, col) for group in range(groups) for col in range(per_group)]
    fetch = [
        (partner(group, col) * per_group + col, group * per_group + col) for group, col in places
    ]
    other_first = lax.ppermute(own[:early], both, fetch)
    other_later = lax.ppermute(own[early:], both, fetch)
    left, own_right, own_dir, factors = call(
        own_kernel,
        [
            array(group_pts, depth, dtype=bf16),
            array(depth, group_pts, dtype=bf16),
            array(16, group_pts, dtype=bf16),
            array(8, 128),
        ],
        outputscale, noise, own,
        smem=2,
    )
    place = jnp.stack([lax.axis_index("row"), lax.axis_index("col")]).astype(jnp.int32)
    tile = pltpu.VMEM((width, width), bf16)

    def pair_call(blocks, inner_from, turns, tiles, *args):
        def body(*refs):
            pair_kernel(blocks, inner_from, turns, *refs)

        pairs = tiles * width * width
        pts = group_pts + blocks * width
        return call(
            body,
            [array(per_group, 8, width), array(per_group if len(args) > 1 else blocks, 8, width)]
            + ([] if len(args) > 1 else [array(width, width, dtype=bf16)] * 2),
            place, left, own_right, own_dir, *args,
            smem=1,
            scratch=[
                pltpu.VMEM((depth, pts), bf16),
                pltpu.VMEM((16, pts), bf16),
                pltpu.VMEM((16, pts), f32),
                *([tile] * (4 if len(args) > 1 else 2)),
            ],
            limit=32 << 20,
            cost=pl.CostEstimate(
                flops=256 * pairs, transcendentals=2 * pairs, bytes_accessed=1 << 21
            ),
        )

    own_first, out_first, top, low = pair_call(early, 7, first_turns, 16, other_first)
    own_all, out_all = pair_call(
        per_group - early, 16, later_turns, 49, other_later, own_first, out_first, top, low
    )
    back = lax.ppermute(out_all, both, [(to, source) for source, to in fetch])
    total = call(add_kernel, array(per_group, 8, width), own_all, back)
    parts = lax.all_to_all(total, "col", split_axis=0, concat_axis=0)
    image, sums = call(
        image_kernel,
        [array(8, width), array(groups * per_group, 128)],
        factors, parts, direction, residual,
    )
    sums = lax.all_to_all(sums, both, split_axis=0, concat_axis=0, tiled=True)
    return tuple(
        call(
            update_kernel,
            [array(8, width)] * 3,
            sums, image, solution, residual, direction,
        )
    )


def solution(mesh):
    spread = P(None, both)
    return jax.shard_map(
        shards,
        mesh=mesh,
        in_specs=(spread, P(), P(), P(), spread, spread, spread),
        out_specs=(spread, spread, spread),
        check_vma=False,
    )
```

```python
import jax
import jax.numpy as jnp
from jax import lax
from jax.experimental import pallas as pl
from jax.experimental.pallas import tpu as pltpu
from jax.sharding import PartitionSpec as P

width = 512
per_group = 8
groups = 16
early = 2
group_pts = width * per_group
depth = 64
chunk = 128
half_col = 4
pts_scale = 5.0**0.5 / 3.0
f32, bf16 = jnp.float32, jnp.bfloat16
nt_dims = (((1,), (1,)), ((), ()))
both = ("row", "col")


def dot(left, right):
    return jnp.dot(left, right, preferred_element_type=f32)


def split(value, parts):
    out = []
    for _ in range(parts):
        top = value.astype(bf16).astype(f32)
        out.append(top)
        value = value - top
    return out


def send_kernel(pts_hbm, len_hbm, dir_hbm, out_ref, pts_ref, len_ref, dir_ref, sems):
    pairs = ((pts_hbm, pts_ref), (len_hbm, len_ref), (dir_hbm, dir_ref))
    copies = [pltpu.make_async_copy(*pair, sems.at[i]) for i, pair in enumerate(pairs)]
    for copy in copies:
        copy.start()
    for copy in copies:
        copy.wait()
    scaled = pts_ref[...] / lengths_of(len_ref) * pts_scale
    direction = dir_ref[...]
    for block in range(per_group):
        out_ref[block, 0:8, :] = scaled
        out_ref[block, 8:16, :] = direction


def lengths_of(len_ref):
    rows = lax.broadcasted_iota(jnp.int32, (8, width), 0)
    lengths = jnp.zeros((8, width), f32)
    for feat in range(8):
        lengths = jnp.where(rows == feat, len_ref[feat], lengths)
    return lengths


def add_kernel(one_ref, two_ref, out_ref):
    out_ref[...] = one_ref[...] + two_ref[...]


def norm_rows(pts, first):
    rows = lax.broadcasted_iota(jnp.int32, pts.shape, 0)
    out = jnp.where(rows < 6, 1.0, 0.0)
    for i, part in enumerate(split(jnp.sum(pts * pts, axis=0, keepdims=True), 3)):
        out = jnp.where(rows == first + i, part, out)
    return out


def right_rows(pts):
    one, two, three = split(pts, 3)
    return jnp.concatenate(
        [one, two, one, three, two, one, norm_rows(pts, 3), jnp.zeros_like(pts)], axis=0
    )


def left_rows(pts):
    one, two, three = split(pts * -2.0, 3)
    return jnp.concatenate(
        [one, one, two, one, two, three, norm_rows(pts, 0), jnp.zeros_like(pts)], axis=0
    )


def right_and_dir(pts, direction, right_ref, dir_ref, at):
    cols = slice(at * width, (at + 1) * width)
    right_ref[:, cols] = right_rows(pts).astype(bf16)
    dir_ref[:, cols] = jnp.concatenate(split(direction, 2), axis=0).astype(bf16)


def own_kernel(scale_ref, noise_ref, own_ref, left_ref, right_ref, dir_ref, factor_ref):
    rows = lax.broadcasted_iota(jnp.int32, factor_ref.shape, 0)
    factor_ref[...] = jnp.where(rows == 0, 3.0 * scale_ref[0], noise_ref[0])
    for at in range(per_group):
        pts = own_ref[at, 0:8, :]
        left_ref[at * width : (at + 1) * width, :] = left_rows(pts).T.astype(bf16)
        right_and_dir(pts, own_ref[at, 8:16, :], right_ref, dir_ref, at)


def matern(dist):
    dist = jnp.maximum(dist, 1e-30)
    radius = dist * lax.rsqrt(dist)
    decay = jnp.exp2(radius * (-3.0 / 0.6931471805599453))
    return ((dist + 1.0 / 3.0) + radius) * decay


def tile_of(step, group, col, blocks, alone_from, inner_from):
    halved = col == half_col
    pairs = jnp.where(halved, 4 * blocks, 8 * blocks)
    pair_row = step % 8
    pair_col = 8 + jnp.where(halved, 2 * (step // 8) + (pair_row + group // 8) % 2, step // 8)
    inner = step - pairs + jnp.where(halved, inner_from, jnp.where(col > half_col, col - 1, col))
    alone = inner >= alone_from
    row = jnp.where(alone, inner - alone_from, inner % 8)
    column = jnp.where(alone, row, (row + 1 + inner // 8) % 8)
    mixed = step < pairs
    return (
        jnp.where(mixed, pair_row, row),
        jnp.where(mixed, pair_col, column),
        jnp.where(jnp.logical_and(alone, jnp.logical_not(mixed)), 0.5, 1.0),
    )


def pair_kernel(blocks, inner_from, turns, place_ref, left_ref, own_right_ref, own_dir_ref, other_ref, *refs):
    before_ref = None
    if len(refs) == 13:
        before_ref, first_ref, top_in, low_in, *refs = refs
        own_out, other_out, right_ref, dir_ref, acc_ref, top_odd, low_odd, top_even, low_even = refs
    else:
        own_out, other_out, top_even, low_even, right_ref, dir_ref, acc_ref, top_odd, low_odd = refs
    group, col = place_ref[0], place_ref[1]
    halved = col == half_col
    right_ref[:, :group_pts] = own_right_ref[...]
    dir_ref[:, :group_pts] = own_dir_ref[...]
    for at in range(blocks):
        right_and_dir(other_ref[at, 0:8, :], other_ref[at, 8:16, :], right_ref, dir_ref, per_group + at)
    acc_ref[...] = jnp.zeros_like(acc_ref)
    if before_ref is not None:
        for at in range(per_group):
            acc_ref[0:8, at * width : (at + 1) * width] = before_ref[at]

    def place_of(step):
        if before_ref is None:
            row, column, weight = tile_of(step, group, col, blocks, 28, inner_from)
        else:
            handed = tile_of(16, group, col, early, 28, 7)
            later = tile_of(step - 1, group, col, blocks, 28, inner_from)
            row, column, weight = (
                jnp.where(step == 0, one, two) for one, two in zip(handed, later, strict=True)
            )
        return pl.multiple_of(row * width, width), pl.multiple_of(column * width, width), weight

    def evaluate(step, top, low):
        row, column, _ = place_of(step)

        def part(at):
            rows = slice(at * chunk, (at + 1) * chunk)
            tile = matern(
                dot(left_ref[pl.ds(row + at * chunk, chunk), :], right_ref[:, pl.ds(column, width)])
            )
            high = tile.astype(bf16)
            top[rows, :] = high
            low[rows, :] = (tile - high.astype(f32)).astype(bf16)

        return [lambda at=at: part(at) for at in range(width // chunk)]

    def multiply(step, top, low):
        row, column, weight = place_of(step)

        def to_column(tile):
            acc_ref[:, pl.ds(column, width)] += weight * dot(
                dir_ref[:, pl.ds(row, width)], tile[...]
            )

        def to_row(tile):
            acc_ref[:, pl.ds(row, width)] += weight * lax.dot_general(
                dir_ref[:, pl.ds(column, width)], tile[...], nt_dims, preferred_element_type=f32
            )

        return [
            lambda: to_row(top), lambda: to_column(top), lambda: to_row(low), lambda: to_column(low)
        ]

    def run(first, second):
        for one, two in zip(first, second, strict=True):
            one()
            two()

    if before_ref is None:
        for part in evaluate(0, top_even, low_even):
            part()
    else:
        top_even[...] = top_in[...]
        low_even[...] = low_in[...]

    def turn(index, carry):
        step = 2 * index
        run(evaluate(step + 1, top_odd, low_odd), multiply(step, top_even, low_even))
        run(evaluate(step + 2, top_even, low_even), multiply(step + 1, top_odd, low_odd))
        return carry

    turns(halved, turn, evaluate, multiply, run, (top_even, low_even), (top_odd, low_odd))
    for at in range(per_group):
        cols = slice(at * width, (at + 1) * width)
        own_out[at] = acc_ref[0:8, cols] + acc_ref[8:16, cols]
    if before_ref is not None:
        other_out[0:early] = first_ref[...]
    for at in range(blocks):
        cols = slice(group_pts + at * width, group_pts + (at + 1) * width)
        other_out[at + other_out.shape[0] - blocks] = acc_ref[0:8, cols] + acc_ref[8:16, cols]


def first_turns(halved, turn, evaluate, multiply, run, even, odd):
    lax.fori_loop(0, 8, turn, 0, unroll=4)


def later_turns(halved, turn, evaluate, multiply, run, even, odd):
    def two_turns(index, carry):
        return turn(2 * index + 1, turn(2 * index, carry))

    def four_turns(index, carry):
        return two_turns(2 * index + 1, two_turns(2 * index, carry))

    lax.fori_loop(0, jnp.where(halved, 5, 6), four_turns, 0)
    lax.fori_loop(10, jnp.where(halved, 11, 10), two_turns, 0)
    for part in multiply(jnp.where(halved, 44, 48), *even):
        part()


def image_kernel(factor_ref, parts_ref, dir_ref, res_ref, image_ref, sums_ref):
    product = parts_ref[0]
    for at in range(1, per_group):
        product = product + parts_ref[at]
    direction, residual = dir_ref[...], res_ref[...]
    image = factor_ref[0:1, 0:1] * product + factor_ref[1:2, 0:1] * direction
    image_ref[...] = image
    rows = lax.broadcasted_iota(jnp.int32, (8, 128), 0)
    lanes = lax.broadcasted_iota(jnp.int32, (8, 128), 1)
    packed = jnp.zeros((8, 128), f32)
    pairs = ((residual, residual), (direction, image), (residual, image), (image, image))
    for i, (one, two) in enumerate(pairs):
        packed = jnp.where(lanes == 8 * i + rows, jnp.sum(one * two, axis=1, keepdims=True), packed)
    sums_ref[...] = jnp.broadcast_to(jnp.sum(packed, axis=0, keepdims=True), sums_ref.shape)


def update_kernel(sums_ref, image_ref, sol_ref, res_ref, dir_ref, new_sol, new_res, new_dir):
    total = jnp.sum(sums_ref[...], axis=0, keepdims=True)
    rows = lax.broadcasted_iota(jnp.int32, (8, 128), 0)
    lanes = lax.broadcasted_iota(jnp.int32, (8, 128), 1)
    rr_old, curv, res_image, image_sq = (
        jnp.sum(jnp.where(lanes == 8 * i + rows, total, 0.0), axis=1, keepdims=True)
        for i in range(4)
    )
    alpha = rr_old / curv
    rr_new = rr_old - alpha * (2.0 * res_image - alpha * image_sq)
    direction = dir_ref[...]
    residual = res_ref[...] - alpha * image_ref[...]
    new_sol[...] = sol_ref[...] + alpha * direction
    new_res[...] = residual
    new_dir[...] = residual + (rr_new / rr_old) * direction


def call(kernel, outs, *args, smem=0, scratch=(), limit=16 << 20, cost=None):
    vmem, scalars = pl.BlockSpec(memory_space=pltpu.VMEM), pl.BlockSpec(memory_space=pltpu.SMEM)
    many = isinstance(outs, list)
    return pl.pallas_call(
        kernel,
        out_shape=outs,
        in_specs=[scalars if i < smem else vmem for i in range(len(args))],
        out_specs=[vmem] * len(outs) if many else vmem,
        scratch_shapes=scratch,
        cost_estimate=cost,
        compiler_params=pltpu.CompilerParams(vmem_limit_bytes=limit),
    )(*args)


def shards(points, lengthscale, outputscale, noise, solution, residual, direction):
    def array(*shape, dtype=f32):
        return jax.ShapeDtypeStruct(shape, dtype)

    def partner(group, col):
        z, x = divmod(group, 4)
        if col == 5:
            dz, dx = ((0, 2), (2, 0))[(z // 2 + x // 2 + 1) % 2]
        else:
            dz, dx = {0: (0, 1), 1: (1, 0), 2: (-2, -1), 3: (1, 1), 4: (2, 2), 6: (-1, -2), 7: (1, -1)}[col]
        return (z + dz) % 4 * 4 + (x + dx) % 4

    sent = pl.pallas_call(
        send_kernel,
        out_shape=array(per_group, 16, width),
        in_specs=[pl.BlockSpec(memory_space=pltpu.HBM)] * 3,
        out_specs=pl.BlockSpec(memory_space=pltpu.VMEM),
        scratch_shapes=[
            pltpu.VMEM((8, width), f32),
            pltpu.SMEM((8,), f32),
            pltpu.VMEM((8, width), f32),
            pltpu.SemaphoreType.DMA((3,)),
        ],
        compiler_params=pltpu.CompilerParams(vmem_limit_bytes=62 << 20),
    )(points, lengthscale, direction)
    own = lax.all_to_all(sent, "col", split_axis=0, concat_axis=0)
    places = [(group, col) for group in range(groups) for col in range(per_group)]
    fetch = [
        (partner(group, col) * per_group + col, group * per_group + col) for group, col in places
    ]
    other_first = lax.ppermute(own[:early], both, fetch)
    other_later = lax.ppermute(own[early:], both, fetch)
    left, own_right, own_dir, factors = call(
        own_kernel,
        [
            array(group_pts, depth, dtype=bf16),
            array(depth, group_pts, dtype=bf16),
            array(16, group_pts, dtype=bf16),
            array(8, 128),
        ],
        outputscale, noise, own,
        smem=2,
    )
    place = jnp.stack([lax.axis_index("row"), lax.axis_index("col")]).astype(jnp.int32)
    tile = pltpu.VMEM((width, width), bf16)

    def pair_call(blocks, inner_from, turns, tiles, *args):
        def body(*refs):
            pair_kernel(blocks, inner_from, turns, *refs)

        pairs = tiles * width * width
        pts = group_pts + blocks * width
        return call(
            body,
            [array(per_group, 8, width), array(per_group if len(args) > 1 else blocks, 8, width)]
            + ([] if len(args) > 1 else [array(width, width, dtype=bf16)] * 2),
            place, left, own_right, own_dir, *args,
            smem=1,
            scratch=[
                pltpu.VMEM((depth, pts), bf16),
                pltpu.VMEM((16, pts), bf16),
                pltpu.VMEM((16, pts), f32),
                *([tile] * (4 if len(args) > 1 else 2)),
            ],
            limit=32 << 20,
            cost=pl.CostEstimate(
                flops=256 * pairs, transcendentals=2 * pairs, bytes_accessed=1 << 21
            ),
        )

    own_first, out_first, top, low = pair_call(early, 7, first_turns, 16, other_first)
    own_all, out_all = pair_call(
        per_group - early, 16, later_turns, 49, other_later, own_first, out_first, top, low
    )
    back = lax.ppermute(out_all, both, [(to, source) for source, to in fetch])
    total = call(add_kernel, array(per_group, 8, width), own_all, back)
    parts = lax.all_to_all(total, "col", split_axis=0, concat_axis=0)
    image, sums = call(
        image_kernel,
        [array(8, width), array(groups * per_group, 128)],
        factors, parts, direction, residual,
    )
    sums = lax.all_to_all(sums, both, split_axis=0, concat_axis=0, tiled=True)
    return tuple(
        call(
            update_kernel,
            [array(8, width)] * 3,
            sums, image, solution, residual, direction,
        )
    )


def solution(mesh):
    spread = P(None, both)
    return jax.shard_map(
        shards,
        mesh=mesh,
        in_specs=(spread, P(), P(), P(), spread, spread, spread),
        out_specs=(spread, spread, spread),
        check_vma=False,
    )
```

```python
import jax
import jax.numpy as jnp
from jax import lax
from jax.experimental import pallas as pl
from jax.experimental.pallas import tpu as pltpu
from jax.sharding import PartitionSpec as P

width = 512
per_group = 8
groups = 16
early = 2
group_pts = width * per_group
depth = 64
chunk = 128
half_col = 4
pts_scale = 5.0**0.5 / 3.0
f32, bf16 = jnp.float32, jnp.bfloat16
nt_dims = (((1,), (1,)), ((), ()))
both = ("row", "col")


def dot(left, right):
    return jnp.dot(left, right, preferred_element_type=f32)


def split(value, parts):
    out = []
    for _ in range(parts):
        top = value.astype(bf16).astype(f32)
        out.append(top)
        value = value - top
    return out


def send_kernel(pts_hbm, len_hbm, dir_hbm, out_ref, pts_ref, len_ref, dir_ref, sems):
    pairs = ((pts_hbm, pts_ref), (len_hbm, len_ref), (dir_hbm, dir_ref))
    copies = [pltpu.make_async_copy(*pair, sems.at[i]) for i, pair in enumerate(pairs)]
    for copy in copies:
        copy.start()
    for copy in copies:
        copy.wait()
    scaled = pts_ref[...] / lengths_of(len_ref) * pts_scale
    direction = dir_ref[...]
    for block in range(per_group):
        out_ref[block, 0:8, :] = scaled
        out_ref[block, 8:16, :] = direction


def lengths_of(len_ref):
    rows = lax.broadcasted_iota(jnp.int32, (8, width), 0)
    lengths = jnp.zeros((8, width), f32)
    for feat in range(8):
        lengths = jnp.where(rows == feat, len_ref[feat], lengths)
    return lengths


def add_kernel(one_ref, two_ref, out_ref):
    out_ref[...] = one_ref[...] + two_ref[...]


def norm_rows(pts, first):
    rows = lax.broadcasted_iota(jnp.int32, pts.shape, 0)
    out = jnp.where(rows < 6, 1.0, 0.0)
    for i, part in enumerate(split(jnp.sum(pts * pts, axis=0, keepdims=True), 3)):
        out = jnp.where(rows == first + i, part, out)
    return out


def right_rows(pts):
    one, two, three = split(pts, 3)
    return jnp.concatenate(
        [one, two, one, three, two, one, norm_rows(pts, 3), jnp.zeros_like(pts)], axis=0
    )


def left_rows(pts):
    one, two, three = split(pts * -2.0, 3)
    return jnp.concatenate(
        [one, one, two, one, two, three, norm_rows(pts, 0), jnp.zeros_like(pts)], axis=0
    )


def right_and_dir(pts, direction, right_ref, dir_ref, at):
    cols = slice(at * width, (at + 1) * width)
    right_ref[:, cols] = right_rows(pts).astype(bf16)
    dir_ref[:, cols] = jnp.concatenate(split(direction, 2), axis=0).astype(bf16)


def own_kernel(scale_ref, noise_ref, own_ref, left_ref, right_ref, dir_ref, factor_ref):
    rows = lax.broadcasted_iota(jnp.int32, factor_ref.shape, 0)
    factor_ref[...] = jnp.where(rows == 0, 3.0 * scale_ref[0], noise_ref[0])
    for at in range(per_group):
        pts = own_ref[at, 0:8, :]
        left_ref[at * width : (at + 1) * width, :] = left_rows(pts).T.astype(bf16)
        right_and_dir(pts, own_ref[at, 8:16, :], right_ref, dir_ref, at)


def matern(dist):
    dist = jnp.maximum(dist, 1e-30)
    radius = dist * lax.rsqrt(dist)
    decay = jnp.exp2(radius * (-3.0 / 0.6931471805599453))
    return ((dist + 1.0 / 3.0) + radius) * decay


def tile_of(step, group, col, blocks, alone_from, inner_from):
    halved = col == half_col
    pairs = jnp.where(halved, 4 * blocks, 8 * blocks)
    pair_row = step % 8
    pair_col = 8 + jnp.where(halved, 2 * (step // 8) + (pair_row + group // 8) % 2, step // 8)
    inner = step - pairs + jnp.where(halved, inner_from, jnp.where(col > half_col, col - 1, col))
    alone = inner >= alone_from
    row = jnp.where(alone, inner - alone_from, inner % 8)
    column = jnp.where(alone, row, (row + 1 + inner // 8) % 8)
    mixed = step < pairs
    return (
        jnp.where(mixed, pair_row, row),
        jnp.where(mixed, pair_col, column),
        jnp.where(jnp.logical_and(alone, jnp.logical_not(mixed)), 0.5, 1.0),
    )


def pair_kernel(blocks, inner_from, turns, place_ref, left_ref, own_right_ref, own_dir_ref, other_ref, *refs):
    before_ref = None
    if len(refs) == 13:
        before_ref, first_ref, top_in, low_in, *refs = refs
        own_out, other_out, right_ref, dir_ref, acc_ref, top_odd, low_odd, top_even, low_even = refs
    else:
        own_out, other_out, top_even, low_even, right_ref, dir_ref, acc_ref, top_odd, low_odd = refs
    group, col = place_ref[0], place_ref[1]
    halved = col == half_col
    right_ref[:, :group_pts] = own_right_ref[...]
    dir_ref[:, :group_pts] = own_dir_ref[...]
    for at in range(blocks):
        right_and_dir(other_ref[at, 0:8, :], other_ref[at, 8:16, :], right_ref, dir_ref, per_group + at)
    acc_ref[...] = jnp.zeros_like(acc_ref)
    if before_ref is not None:
        for at in range(per_group):
            acc_ref[0:8, at * width : (at + 1) * width] = before_ref[at]

    def place_of(step):
        if before_ref is None:
            row, column, weight = tile_of(step, group, col, blocks, 28, inner_from)
        else:
            handed = tile_of(16, group, col, early, 28, 7)
            later = tile_of(step - 1, group, col, blocks, 28, inner_from)
            row, column, weight = (
                jnp.where(step == 0, one, two) for one, two in zip(handed, later, strict=True)
            )
        return pl.multiple_of(row * width, width), pl.multiple_of(column * width, width), weight

    def evaluate(step, top, low):
        row, column, _ = place_of(step)

        def part(at):
            rows = slice(at * chunk, (at + 1) * chunk)
            tile = matern(
                dot(left_ref[pl.ds(row + at * chunk, chunk), :], right_ref[:, pl.ds(column, width)])
            )
            high = tile.astype(bf16)
            top[rows, :] = high
            low[rows, :] = (tile - high.astype(f32)).astype(bf16)

        return [lambda at=at: part(at) for at in range(width // chunk)]

    def multiply(step, top, low):
        row, column, weight = place_of(step)

        def to_column(tile):
            acc_ref[:, pl.ds(column, width)] += weight * dot(
                dir_ref[:, pl.ds(row, width)], tile[...]
            )

        def to_row(tile):
            acc_ref[:, pl.ds(row, width)] += weight * lax.dot_general(
                dir_ref[:, pl.ds(column, width)], tile[...], nt_dims, preferred_element_type=f32
            )

        return [
            lambda: to_row(top), lambda: to_column(top), lambda: to_row(low), lambda: to_column(low)
        ]

    def run(first, second):
        for one, two in zip(first, second, strict=True):
            one()
            two()

    if before_ref is None:
        for part in evaluate(0, top_even, low_even):
            part()
    else:
        top_even[...] = top_in[...]
        low_even[...] = low_in[...]

    def turn(index, carry):
        step = 2 * index
        run(evaluate(step + 1, top_odd, low_odd), multiply(step, top_even, low_even))
        run(evaluate(step + 2, top_even, low_even), multiply(step + 1, top_odd, low_odd))
        return carry

    turns(halved, turn, evaluate, multiply, run, (top_even, low_even), (top_odd, low_odd))
    for at in range(per_group):
        cols = slice(at * width, (at + 1) * width)
        own_out[at] = acc_ref[0:8, cols] + acc_ref[8:16, cols]
    if before_ref is not None:
        other_out[0:early] = first_ref[...]
    for at in range(blocks):
        cols = slice(group_pts + at * width, group_pts + (at + 1) * width)
        other_out[at + other_out.shape[0] - blocks] = acc_ref[0:8, cols] + acc_ref[8:16, cols]


def first_turns(halved, turn, evaluate, multiply, run, even, odd):
    lax.fori_loop(0, 8, turn, 0, unroll=4)


def later_turns(halved, turn, evaluate, multiply, run, even, odd):
    def two_turns(index, carry):
        return turn(2 * index + 1, turn(2 * index, carry))

    def four_turns(index, carry):
        return two_turns(2 * index + 1, two_turns(2 * index, carry))

    lax.fori_loop(0, jnp.where(halved, 5, 6), four_turns, 0)
    lax.fori_loop(10, jnp.where(halved, 11, 10), two_turns, 0)
    for part in multiply(jnp.where(halved, 44, 48), *even):
        part()


def image_kernel(factor_ref, parts_ref, dir_ref, res_ref, image_ref, sums_ref):
    product = parts_ref[0]
    for at in range(1, per_group):
        product = product + parts_ref[at]
    direction, residual = dir_ref[...], res_ref[...]
    image = factor_ref[0:1, 0:1] * product + factor_ref[1:2, 0:1] * direction
    image_ref[...] = image
    rows = lax.broadcasted_iota(jnp.int32, (8, 128), 0)
    lanes = lax.broadcasted_iota(jnp.int32, (8, 128), 1)
    packed = jnp.zeros((8, 128), f32)
    pairs = ((residual, residual), (direction, image), (residual, image), (image, image))
    for i, (one, two) in enumerate(pairs):
        packed = jnp.where(lanes == 8 * i + rows, jnp.sum(one * two, axis=1, keepdims=True), packed)
    sums_ref[...] = jnp.broadcast_to(jnp.sum(packed, axis=0, keepdims=True), sums_ref.shape)


def update_kernel(sums_ref, image_ref, sol_ref, res_ref, dir_ref, new_sol, new_res, new_dir):
    total = jnp.sum(sums_ref[...], axis=0, keepdims=True)
    rows = lax.broadcasted_iota(jnp.int32, (8, 128), 0)
    lanes = lax.broadcasted_iota(jnp.int32, (8, 128), 1)
    rr_old, curv, res_image, image_sq = (
        jnp.sum(jnp.where(lanes == 8 * i + rows, total, 0.0), axis=1, keepdims=True)
        for i in range(4)
    )
    alpha = rr_old / curv
    rr_new = rr_old - alpha * (2.0 * res_image - alpha * image_sq)
    direction = dir_ref[...]
    residual = res_ref[...] - alpha * image_ref[...]
    new_sol[...] = sol_ref[...] + alpha * direction
    new_res[...] = residual
    new_dir[...] = residual + (rr_new / rr_old) * direction


def call(kernel, outs, *args, smem=0, scratch=(), limit=16 << 20, cost=None):
    vmem, scalars = pl.BlockSpec(memory_space=pltpu.VMEM), pl.BlockSpec(memory_space=pltpu.SMEM)
    many = isinstance(outs, list)
    return pl.pallas_call(
        kernel,
        out_shape=outs,
        in_specs=[scalars if i < smem else vmem for i in range(len(args))],
        out_specs=[vmem] * len(outs) if many else vmem,
        scratch_shapes=scratch,
        cost_estimate=cost,
        compiler_params=pltpu.CompilerParams(vmem_limit_bytes=limit),
    )(*args)


def shards(points, lengthscale, outputscale, noise, solution, residual, direction):
    def array(*shape, dtype=f32):
        return jax.ShapeDtypeStruct(shape, dtype)

    def partner(group, col):
        z, x = divmod(group, 4)
        if col == 1:
            dz, dx = ((0, 2), (2, 0))[(z // 2 + x // 2 + 1) % 2]
        else:
            dz, dx = {4: (-2, -2), 5: (0, 1), 6: (-1, -2), 7: (1, 0), 2: (-2, -1), 3: (-1, -1), 0: (-1, 1)}[col]
        return (z + dz) % 4 * 4 + (x + dx) % 4

    sent = pl.pallas_call(
        send_kernel,
        out_shape=array(per_group, 16, width),
        in_specs=[pl.BlockSpec(memory_space=pltpu.HBM)] * 3,
        out_specs=pl.BlockSpec(memory_space=pltpu.VMEM),
        scratch_shapes=[
            pltpu.VMEM((8, width), f32),
            pltpu.SMEM((8,), f32),
            pltpu.VMEM((8, width), f32),
            pltpu.SemaphoreType.DMA((3,)),
        ],
        compiler_params=pltpu.CompilerParams(vmem_limit_bytes=62 << 20),
    )(points, lengthscale, direction)
    own = lax.all_to_all(sent, "col", split_axis=0, concat_axis=0)
    places = [(group, col) for group in range(groups) for col in range(per_group)]
    fetch = [
        (partner(group, col) * per_group + col, group * per_group + col) for group, col in places
    ]
    other_first = lax.ppermute(own[:early], both, fetch)
    other_later = lax.ppermute(own[early:], both, fetch)
    left, own_right, own_dir, factors = call(
        own_kernel,
        [
            array(group_pts, depth, dtype=bf16),
            array(depth, group_pts, dtype=bf16),
            array(16, group_pts, dtype=bf16),
            array(8, 128),
        ],
        outputscale, noise, own,
        smem=2,
    )
    place = jnp.stack([lax.axis_index("row"), lax.axis_index("col")]).astype(jnp.int32)
    tile = pltpu.VMEM((width, width), bf16)

    def pair_call(blocks, inner_from, turns, tiles, *args):
        def body(*refs):
            pair_kernel(blocks, inner_from, turns, *refs)

        pairs = tiles * width * width
        pts = group_pts + blocks * width
        return call(
            body,
            [array(per_group, 8, width), array(per_group if len(args) > 1 else blocks, 8, width)]
            + ([] if len(args) > 1 else [array(width, width, dtype=bf16)] * 2),
            place, left, own_right, own_dir, *args,
            smem=1,
            scratch=[
                pltpu.VMEM((depth, pts), bf16),
                pltpu.VMEM((16, pts), bf16),
                pltpu.VMEM((16, pts), f32),
                *([tile] * (4 if len(args) > 1 else 2)),
            ],
            limit=32 << 20,
            cost=pl.CostEstimate(
                flops=256 * pairs, transcendentals=2 * pairs, bytes_accessed=1 << 21
            ),
        )

    own_first, out_first, top, low = pair_call(early, 7, first_turns, 16, other_first)
    own_all, out_all = pair_call(
        per_group - early, 16, later_turns, 49, other_later, own_first, out_first, top, low
    )
    back = lax.ppermute(out_all, both, [(to, source) for source, to in fetch])
    total = call(add_kernel, array(per_group, 8, width), own_all, back)
    parts = lax.all_to_all(total, "col", split_axis=0, concat_axis=0)
    image, sums = call(
        image_kernel,
        [array(8, width), array(groups * per_group, 128)],
        factors, parts, direction, residual,
    )
    sums = lax.all_to_all(sums, both, split_axis=0, concat_axis=0, tiled=True)
    return tuple(
        call(
            update_kernel,
            [array(8, width)] * 3,
            sums, image, solution, residual, direction,
        )
    )


def solution(mesh):
    spread = P(None, both)
    return jax.shard_map(
        shards,
        mesh=mesh,
        in_specs=(spread, P(), P(), P(), spread, spread, spread),
        out_specs=(spread, spread, spread),
        check_vma=False,
    )
```
